32 devices in a mesh: lat: 16 (over z, y, x), wid: 2 (over core).
Axes of the slice: x: 2, y: 2, z: 4, core: 2. Of those that a mesh axis runs over, the one named last changes fastest.
Arguments:
- activations: bfloat16 [128, 3584], P(None, 'wid'), may hold values from -6 to 6
- encoder: bfloat16 [3584, 8192], P('wid', 'lat'), may hold values from -0.09375 to 0.09375
- encoder_bias: float32 [8192], P('lat'), may hold values from -3 to 3
- decoder: bfloat16 [8192, 3584], P('lat', 'wid'), may hold values from -0.75 to 0.75
- decoder_bias: float32 [3584], P('wid'), may hold values from -3 to 3
- kept_mask: int32 [128, 8192], P(None, 'lat'), may hold values 0 or 1
- boundaries: int32 [8], replicated, may hold values from 1025 to 8192, as said below
Outputs:
- encoder_grad: bfloat16 [3584, 8192], P('wid', 'lat')
- encoder_bias_grad: float32 [8192], P('lat')
- decoder_grad: bfloat16 [8192, 3584], P('lat', 'wid')
- decoder_bias_grad: float32 [3584], P('wid')
The draws below stay inside these ranges and needn't reach their ends.
Inputs may be any that keep to these rules, and one draw needn't show every extreme that they name: `boundaries`: Rising; for k below 7, boundary k lies among the 512 latents that follow (k + 1) * 1024; the last equals 8192.
All inputs are finite; a program needn't handle non-finite values. No bound on the sum of `kept_mask` on one device may be relied on, other than what follows from the above.
Results may differ from the reference program's by a relative error of at most 0.006.
Values may be sent and summed in bfloat16 or wider, within the bound.
A program may use at most 128 MiB of HBM per device.

```python
import jax
import jax.numpy as jnp
from jax import lax

D = 3584
LAT_DEV = 512
TOKENS = 128
GROUPS = 8
KEEP = 64
LATENTS = 8192
N_LAT = 16


def draw_boundaries(key, part):
    span_width = LATENTS // GROUPS
    jitter = jax.random.randint(key, (GROUPS,), 0, LAT_DEV)
    range_starts = jnp.arange(1, GROUPS + 1, dtype=jnp.int32) * span_width
    final_slot = jnp.arange(GROUPS) == GROUPS - 1
    return jnp.where(final_slot, LATENTS, range_starts + 1 + jitter).astype(jnp.int32)


def plant(array, rng, low, top_value):
    shape = array.shape
    index_at = [jax.random.randint(jax.random.fold_in(rng, axis), (), 0, shape[axis]) for axis in range(len(shape))]
    array = array.at[tuple(index_at)].set(low)
    longest = shape.index(max(shape))
    index_at[longest] = (index_at[longest] + 1) % shape[longest]
    return array.at[tuple(index_at)].set(top_value)


def shard_levels(key, extent, cuts, smallest, top_value):
    def one(axis_at, blocks):
        draws = jax.random.uniform(jax.random.fold_in(jax.random.fold_in(key, 6), axis_at), (blocks,), jnp.float32, smallest / len(cuts), top_value / len(cuts))
        return jnp.repeat(jnp.exp(draws), extent[axis_at] // blocks).reshape((-1,) + (1,) * (len(extent) - axis_at - 1))

    loudness = one(*cuts[0])
    for cut in cuts[1:]:
        loudness = loudness * one(*cut)
    return loudness


def noise(own_key, dims, scale, limit, shards=(), kind=jnp.bfloat16):
    array = scale * jax.random.normal(own_key, dims, jnp.float32)
    if shards:
        array = array * shard_levels(own_key, dims, shards, -0.22, 0.18)
    return jnp.clip(array, -limit, limit).astype(kind)


def setup_inputs(seed: int = 0) -> dict:
    keys = jax.random.split(jax.random.key(seed), 8)
    activations = noise(keys[0], (TOKENS, D), 1.0, 6.0, ((1, 2),))
    encoder = noise(keys[1], (D, LATENTS), D ** -0.5, 0.09375, ((0, 2), (1, 16)))
    encoder_bias = noise(keys[2], (LATENTS,), 0.5, 3.0, ((0, 16),), jnp.float32)
    decoder = noise(keys[3], (LATENTS, D), KEEP ** -0.5, 0.75, ((0, 16), (1, 2)))
    decoder_bias = noise(keys[4], (D,), 0.5, 3.0, ((0, 2),), jnp.float32)
    kept_mask = plant((jax.random.randint(keys[5], (TOKENS, LATENTS), 0, LATENTS) < KEEP).astype(jnp.int32), jax.random.fold_in(keys[5], 1), 0, 1)
    boundaries = draw_boundaries(jax.random.fold_in(keys[7], 71), 0)
    return {"activations": activations, "encoder": encoder, "encoder_bias": encoder_bias, "decoder": decoder, "decoder_bias": decoder_bias, "kept_mask": kept_mask, "boundaries": boundaries}


def block_product(operands):
    return jnp.dot(operands[0], operands[1], preferred_element_type=jnp.float32)


def block_back(operands):
    return jnp.dot(operands[0], operands[1].T, preferred_element_type=jnp.float32)


def block_outer(operands):
    return jnp.dot(operands[0].T, operands[1], preferred_element_type=jnp.float32)


def reference(activations, encoder, encoder_bias, decoder, decoder_bias, kept_mask, boundaries):
    preacts = jnp.dot(activations, encoder, preferred_element_type=jnp.float32) + encoder_bias
    kept_float = kept_mask.astype(jnp.float32)
    codes = (kept_float * preacts).astype(jnp.bfloat16)
    code_blocks = jnp.transpose(codes.reshape(TOKENS, N_LAT, LAT_DEV), (1, 0, 2))
    decoder_blocks = decoder.reshape(N_LAT, LAT_DEV, D)
    totals = lax.map(block_product, (code_blocks, decoder_blocks))
    earlier = jnp.concatenate([jnp.zeros((1, TOKENS, D), jnp.float32), jnp.cumsum(totals, axis=0)[:-1]], axis=0)
    local_ids = jnp.arange(LAT_DEV, dtype=jnp.int32)
    target_rows = activations.astype(jnp.float32)
    error_list = []
    for boundary in range(GROUPS):
        cut_point = boundaries[boundary].astype(jnp.int32)
        block_index = ((cut_point - 1) // LAT_DEV).astype(jnp.int32)
        block_codes = lax.dynamic_index_in_dim(code_blocks, block_index, 0, keepdims=False)
        block_decoder = lax.dynamic_index_in_dim(decoder_blocks, block_index, 0, keepdims=False)
        below_cut = (block_index * LAT_DEV + local_ids) < cut_point
        masked_codes = jnp.where(below_cut[None, :], block_codes, jnp.zeros((), jnp.bfloat16))
        recon = decoder_bias + earlier[block_index] + block_product((masked_codes, block_decoder))
        error_list.append(recon - target_rows)
    errors = jnp.stack(error_list)
    suffix = jnp.cumsum(errors[::-1], axis=0)[::-1] / GROUPS
    suffix_low = suffix.astype(jnp.bfloat16)
    padded = jnp.concatenate([suffix_low, jnp.zeros((1, TOKENS, D), jnp.bfloat16)], axis=0)
    block_starts = jnp.arange(N_LAT, dtype=jnp.int32) * LAT_DEV
    start_group = jnp.sum((boundaries[None, :] <= block_starts[:, None]).astype(jnp.int32), axis=1)
    block_suffix = padded[start_group]
    code_grads = lax.map(block_back, (block_suffix, decoder_blocks))
    decoder_grads = lax.map(block_outer, (code_blocks, block_suffix))
    for boundary in range(GROUPS):
        cut_point = boundaries[boundary].astype(jnp.int32)
        block_index = ((cut_point - 1) // LAT_DEV).astype(jnp.int32)
        block_codes = lax.dynamic_index_in_dim(code_blocks, block_index, 0, keepdims=False)
        block_decoder = lax.dynamic_index_in_dim(decoder_blocks, block_index, 0, keepdims=False)
        above_cut = (block_index * LAT_DEV + local_ids) >= cut_point
        later_suffix = padded[boundary + 1]
        fixed_codes = jnp.where(above_cut[None, :], block_back((later_suffix, block_decoder)), code_grads[block_index])
        code_grads = code_grads.at[block_index].set(fixed_codes)
        fixed_rows = jnp.where(above_cut[:, None], block_outer((block_codes, later_suffix)), decoder_grads[block_index])
        decoder_grads = decoder_grads.at[block_index].set(fixed_rows)
    code_grad_all = jnp.transpose(code_grads, (1, 0, 2)).reshape(TOKENS, LATENTS)
    pre_grads = kept_float * code_grad_all
    encoder_bias_grad = jnp.sum(pre_grads, axis=0)
    encoder_grad = jnp.dot(activations.T, pre_grads.astype(jnp.bfloat16), preferred_element_type=jnp.float32).astype(jnp.bfloat16)
    decoder_grad = decoder_grads.reshape(LATENTS, D).astype(jnp.bfloat16)
    decoder_bias_grad = jnp.sum(suffix[0], axis=0)
    return (encoder_grad, encoder_bias_grad, decoder_grad, decoder_bias_grad)
```

```python
import functools

import jax
import jax.numpy as jnp
from jax import lax
from jax.experimental import pallas as pl
from jax.experimental.pallas import tpu as pltpu
from jax.sharding import PartitionSpec as P

GROUPS = 8
HALF = 8
SUB = 16
CHUNKS = 2
MESH = pl.DeviceIdType.MESH


def prefix(part, axis, combine, identity, reverse):
    count = lax.axis_size(axis)
    place = lax.axis_index(axis)
    ahead = count - 1 - place if reverse else place
    gathered = lax.all_gather(part, axis)
    state = jnp.zeros_like(part) + jnp.asarray(identity, part.dtype)

    def one(step, state):
        source = count - 1 - step if reverse else step
        return combine(state, lax.dynamic_index_in_dim(gathered, source, 0, False))

    return lax.fori_loop(0, ahead, one, state)


def add_terms(earlier, later):
    return earlier + later


def general_body(activations, encoder, encoder_bias, decoder, decoder_bias, kept_mask, boundaries):
    latent_width = encoder.shape[1]
    first_latent = lax.axis_index("lat") * latent_width
    latent_ids = first_latent + jnp.arange(latent_width, dtype=jnp.int32)
    kept_float = kept_mask.astype(jnp.float32)
    encoder_part = jnp.dot(activations, encoder, preferred_element_type=jnp.float32)
    preacts = lax.psum(encoder_part, "wid") + encoder_bias
    codes = (kept_float * preacts).astype(jnp.bfloat16)
    inside_rows = (boundaries > first_latent) & (boundaries <= first_latent + latent_width)
    holds_cut = jnp.any(inside_rows)
    cut_point = jnp.sum(jnp.where(inside_rows, boundaries, 0))
    below_cut = latent_ids < cut_point
    zero_code = jnp.zeros((), jnp.bfloat16)
    masked_codes = jnp.stack(
        [
            jnp.where(below_cut[None, :], codes, zero_code),
            jnp.where(below_cut[None, :], zero_code, codes),
        ]
    )
    decoded_pieces = jnp.einsum(
        "sbj,jd->sbd", masked_codes, decoder, preferred_element_type=jnp.float32
    )
    local_total = decoded_pieces[0] + decoded_pieces[1]
    zero_rows = jnp.zeros_like(local_total)
    prefix_sum = prefix(local_total, "lat", add_terms, zero_rows, False)
    target_rows = activations.astype(jnp.float32)
    scaled_error = jnp.where(
        holds_cut, (decoder_bias + prefix_sum + decoded_pieces[0] - target_rows) / GROUPS, 0.0
    )
    suffix_sum = prefix(scaled_error, "lat", add_terms, zero_rows, True)
    below_suffix = suffix_sum + scaled_error
    suffix_pair = jnp.stack([below_suffix, suffix_sum]).astype(jnp.bfloat16)
    back_grads = jnp.einsum("sbd,jd->sbj", suffix_pair, decoder, preferred_element_type=jnp.float32)
    partial_grads = jnp.where(below_cut[None, :], back_grads[0], back_grads[1])
    coded_grads = lax.psum(partial_grads, "wid")
    pre_grads = kept_float * coded_grads
    encoder_bias_grad = jnp.sum(pre_grads, axis=0)
    pre_low = pre_grads.astype(jnp.bfloat16)
    encoder_grad = lax.dot_general(
        activations, pre_low, (((0,), (0,)), ((), ())), preferred_element_type=jnp.float32
    ).astype(jnp.bfloat16)
    decoder_grad = jnp.einsum(
        "sbj,sbd->jd", masked_codes, suffix_pair, preferred_element_type=jnp.float32
    ).astype(jnp.bfloat16)
    decoder_bias_grad = lax.psum(jnp.sum(scaled_error, axis=0), "lat")
    return (encoder_grad, encoder_bias_grad, decoder_grad, decoder_bias_grad)


def reduce_pieces(pieces, chunk):
    def piece(source, which):
        return pieces[chunk, source, which].astype(jnp.float32)

    upper = [piece(2 * k, 1) + piece(2 * k + 1, 1) for k in range(4)]
    lower = [piece(2 * k, 0) for k in range(4)]
    segments = [upper[k] + lower[k + 1] for k in range(3)] + [upper[3]]
    return lower[0], segments


def exchange_kernel(
    act_hbm, enc_hbm, enc_bias, dec_hbm, dec_bias, mask_hbm, bounds,
    codes_out, suffix_out, pre_out, enc_bias_out, dec_bias_out,
    act, enc, dec, mask, part, part_in, grad, grad_in, codes,
    pieces_out, pieces, cross_out, cross_in, tails, suffix,
    row_out, rows, final_out, final_in,
    load_sems, wid_sems, a_send, a_recv, x_send, x_recv, b_send, b_recv, r_send, r_recv, store_sems,
):
    lat = lax.axis_index("lat")
    wid = lax.axis_index("wid")
    half = lat // HALF
    place = lat % HALF
    even = place % 2 == 0
    odd = place % 2 == 1
    width = act.shape[1]
    wide = width // CHUNKS
    block = dec.shape[0]
    other_core = {"lat": lat, "wid": 1 - wid}
    other_half = {"lat": (lat + HALF) % (2 * HALF), "wid": wid}

    def peer(step):
        return (place + step) % HALF

    def source(step):
        return (place + HALF - step) % HALF

    def device(position):
        return {"lat": half * HALF + position, "wid": wid}

    def remote(src, dst, send, recv, target):
        return pltpu.make_async_remote_copy(
            src_ref=src, dst_ref=dst, send_sem=send, recv_sem=recv, device_id=target, device_id_type=MESH
        )

    barrier = pltpu.get_barrier_semaphore()
    for step in range(1, HALF):
        pl.semaphore_signal(barrier, inc=1, device_id=device(peer(step)), device_id_type=MESH)
    pl.semaphore_signal(barrier, inc=1, device_id=other_core, device_id_type=MESH)
    pl.semaphore_signal(barrier, inc=1, device_id=other_half, device_id_type=MESH)

    load_act = pltpu.make_async_copy(act_hbm, act, load_sems.at[0])
    load_act.start()
    load_enc = []
    for c in range(CHUNKS):
        span = pl.ds(c * wide, wide)
        load_enc.append(pltpu.make_async_copy(enc_hbm.at[span], enc.at[span], load_sems.at[1 + c]))
        load_enc[-1].start()
    load_mask = pltpu.make_async_copy(mask_hbm, mask, load_sems.at[1 + CHUNKS])
    load_mask.start()
    load_dec = pltpu.make_async_copy(dec_hbm, dec, load_sems.at[2 + CHUNKS])
    load_dec.start()

    @pl.when(odd)
    def _():
        for c in range(CHUNKS):
            for r in range(HALF):
                suffix[c, r, 0] = jnp.zeros((SUB, wide), jnp.bfloat16)

    load_act.wait()
    total = None
    for c in range(CHUNKS):
        load_enc[c].wait()
        term = jnp.dot(
            act[:, c * wide : (c + 1) * wide], enc[c * wide : (c + 1) * wide, :], preferred_element_type=jnp.float32
        )
        total = term if total is None else total + term
    part[...] = total
    pl.semaphore_wait(barrier, HALF + 1)
    swap = remote(part, part_in, wid_sems.at[0], wid_sems.at[1], other_core)
    swap.start()

    first = lat * block
    cut = jnp.int32(0)
    for k in range(GROUPS - 1):
        bound = bounds[k]
        cut = cut + jnp.where((bound > first) & (bound <= first + block), bound, 0)
    tokens = act.shape[0]
    below = (lax.broadcasted_iota(jnp.int32, (tokens, block), 1) + first) < cut
    load_mask.wait()
    kept = mask[...].astype(jnp.float32)
    load_dec.wait()
    swap.wait()
    full = kept * ((part[...] + part_in[...]) + enc_bias[...])
    low = jnp.where(below, full, 0.0).astype(jnp.bfloat16)
    high = jnp.where(below, 0.0, full).astype(jnp.bfloat16)
    for r in range(HALF):
        codes[2 * SUB * r : 2 * SUB * r + SUB, :] = low[SUB * r : SUB * (r + 1), :]
        codes[2 * SUB * r + SUB : 2 * SUB * (r + 1), :] = high[SUB * r : SUB * (r + 1), :]
    store_codes = pltpu.make_async_copy(codes, codes_out, store_sems.at[0])
    store_codes.start()

    def send_pieces(c, step, both):
        target = peer(step)
        if both:
            src, dst = pieces_out.at[c, target], pieces.at[c, place]
        else:
            src, dst = pieces_out.at[c, target, 1], pieces.at[c, place, 1]
        return remote(src, dst, a_send.at[c, step], a_recv.at[c, place], device(target))

    def wait_pieces(c, step):
        origin = source(step)

        @pl.when(origin % 2 == 0)
        def _():
            remote(
                pieces_out.at[c, origin], pieces.at[c, origin], a_send.at[c, step], a_recv.at[c, origin], device(origin)
            ).wait_recv()

        @pl.when(origin % 2 == 1)
        def _():
            remote(
                pieces_out.at[c, origin, 1], pieces.at[c, origin, 1], a_send.at[c, step], a_recv.at[c, origin],
                device(origin),
            ).wait_recv()

    for c in range(CHUNKS):
        made = jnp.dot(codes[...], dec[:, c * wide : (c + 1) * wide], preferred_element_type=jnp.float32)
        pieces_out[c] = made.astype(jnp.bfloat16).reshape(HALF, 2, SUB, wide)

        @pl.when(even)
        def _():
            for step in range(1, HALF):
                send_pieces(c, step, True).start()

        @pl.when(odd)
        def _():
            for step in range(1, HALF):
                send_pieces(c, step, False).start()

        pieces[c, place] = pieces_out[c, place]

    crossing = []
    for c in range(CHUNKS):
        for step in range(1, HALF):
            wait_pieces(c, step)
        low0, seg = reduce_pieces(pieces, c)
        plain = ((low0 + seg[0]) + seg[1]) + (seg[2] + seg[3])
        weighted = ((5.0 * low0 + 4.0 * seg[0]) + 3.0 * seg[1]) + (2.0 * seg[2] + seg[3])
        cross_out[c] = jnp.where(half == 0, plain, weighted).astype(jnp.bfloat16)
        crossing.append(remote(cross_out.at[c], cross_in.at[c], x_send.at[c], x_recv.at[c], other_half))
        crossing[-1].start()

    def send_suffix(c, step, both):
        target = peer(step)
        if both:
            src, dst = tails.at[c, pl.ds(target // 2, 2)], suffix.at[c, place]
        else:
            src, dst = tails.at[c, target // 2 + 1], suffix.at[c, place, 1]
        return remote(src, dst, b_send.at[c, step], b_recv.at[c, place], device(target))

    later = half.astype(jnp.float32)
    own_rows = pl.ds(pl.multiple_of(place * SUB, SUB), SUB)
    for c in range(CHUNKS):
        span = slice(c * wide, (c + 1) * wide)
        low0, seg = reduce_pieces(pieces, c)
        crossing[c].wait_recv()
        got = cross_in[c].astype(jnp.float32)
        base = dec_bias[:, span] - act[own_rows, span].astype(jnp.float32)
        before = base + later * (got + low0)
        errors = []
        running = before
        for k in range(4):
            running = running + seg[k]
            errors.append(running)
        tail = jnp.where(half == 0, 5.0 * errors[3] + got, errors[3])
        scaled = [tail]
        for k in (2, 1, 0):
            tail = tail + errors[k]
            scaled.append(tail)
        scaled.append(tail + before)
        for k in range(5):
            tails[c, k] = (scaled[4 - k] / GROUPS).astype(jnp.bfloat16)
        row_out[:, span] = jnp.sum(scaled[3] / GROUPS, axis=0, keepdims=True)
        for step in range(1, HALF):

            @pl.when(peer(step) % 2 == 0)
            def _():
                send_suffix(c, step, True).start()

            @pl.when(peer(step) % 2 == 1)
            def _():
                send_suffix(c, step, False).start()

        suffix[c, place] = tails[c, pl.ds(place // 2, 2)]

    def row_copy(step):
        return remote(row_out, rows.at[place], r_send.at[step], r_recv.at[place], device(peer(step)))

    for step in range(1, HALF):
        row_copy(step).start()
    rows[place] = row_out[...]

    back = None
    stores = []
    for c in range(CHUNKS):

        @pl.when(even)
        def _():
            for step in range(1, HALF):
                origin = source(step)
                remote(
                    suffix.at[c, origin], suffix.at[c, origin], b_send.at[c, step], b_recv.at[c, origin], device(origin)
                ).wait_recv()

        @pl.when(odd)
        def _():
            for step in range(1, HALF):
                origin = source(step)
                remote(
                    suffix.at[c, origin, 1], suffix.at[c, origin, 1], b_send.at[c, step], b_recv.at[c, origin],
                    device(origin),
                ).wait_recv()

        stores.append(pltpu.make_async_copy(suffix.at[c], suffix_out.at[c], store_sems.at[1 + c]))
        stores[-1].start()
        term = lax.dot_general(
            suffix[c].reshape(2 * tokens, wide), dec[:, c * wide : (c + 1) * wide],
            (((1,), (1,)), ((), ())), preferred_element_type=jnp.float32,
        )
        back = term if back is None else back + term
    pair = back.reshape(HALF, 2, SUB, block)
    below_parts = below.astype(jnp.float32).reshape(HALF, SUB, block) > 0.5
    grad[...] = jnp.where(below_parts, pair[:, 0], pair[:, 1]).reshape(tokens, block)
    swap_back = remote(grad, grad_in, wid_sems.at[2], wid_sems.at[3], other_core)
    swap_back.start()

    for step in range(1, HALF):
        origin = source(step)
        remote(row_out, rows.at[origin], r_send.at[step], r_recv.at[origin], device(origin)).wait_recv()
    summed = rows[0]
    for r in range(1, HALF):
        summed = summed + rows[r]
    final_out[...] = summed
    finish = remote(final_out, final_in, x_send.at[CHUNKS], x_recv.at[CHUNKS], other_half)
    finish.start()

    swap_back.wait()
    pre = kept * (grad[...] + grad_in[...])
    enc_bias_out[...] = jnp.sum(pre, axis=0, keepdims=True)
    pre_out[...] = pre.astype(jnp.bfloat16)

    for c in range(CHUNKS):
        crossing[c].wait_send()

        @pl.when(even)
        def _():
            for step in range(1, HALF):
                send_pieces(c, step, True).wait_send()

        @pl.when(odd)
        def _():
            for step in range(1, HALF):
                send_pieces(c, step, False).wait_send()

        for step in range(1, HALF):

            @pl.when(peer(step) % 2 == 0)
            def _():
                send_suffix(c, step, True).wait_send()

            @pl.when(peer(step) % 2 == 1)
            def _():
                send_suffix(c, step, False).wait_send()

    for step in range(1, HALF):
        row_copy(step).wait_send()
    finish.wait()
    dec_bias_out[...] = jnp.where(half == 0, final_out[...], final_in[...])
    store_codes.wait()
    for store in stores:
        store.wait()


def grads_kernel(act, pre, codes, suffix, enc_bias_in, dec_bias_in, enc_grad, dec_grad, enc_bias_out, dec_bias_out):
    contract_rows = (((0,), (0,)), ((), ()))
    enc_grad[...] = lax.dot_general(act[...], pre[...], contract_rows, preferred_element_type=jnp.float32).astype(
        jnp.bfloat16
    )
    dec_grad[...] = lax.dot_general(
        codes[...], suffix[0], contract_rows, preferred_element_type=jnp.float32
    ).astype(jnp.bfloat16)
    enc_bias_out[...] = enc_bias_in[...]
    dec_bias_out[...] = dec_bias_in[...]


def kernel_body(activations, encoder, encoder_bias, decoder, decoder_bias, kept_mask, boundaries):
    tokens, width = activations.shape
    block = encoder.shape[1]
    wide = width // CHUNKS
    low, full = jnp.bfloat16, jnp.float32
    hbm = pl.BlockSpec(memory_space=pl.ANY)
    vmem = pl.BlockSpec(memory_space=pltpu.VMEM)
    smem = pl.BlockSpec(memory_space=pltpu.SMEM)
    dma = pltpu.SemaphoreType.DMA
    codes, suffix, pre, enc_bias_grad, dec_bias_grad = pl.pallas_call(
        exchange_kernel,
        out_shape=[
            jax.ShapeDtypeStruct((2 * tokens, block), low),
            jax.ShapeDtypeStruct((CHUNKS, HALF, 2, SUB, wide), low),
            jax.ShapeDtypeStruct((tokens, block), low),
            jax.ShapeDtypeStruct((1, block), full),
            jax.ShapeDtypeStruct((1, width), full),
        ],
        in_specs=[hbm, hbm, vmem, hbm, vmem, hbm, smem],
        out_specs=[hbm, hbm, vmem, vmem, vmem],
        scratch_shapes=[
            pltpu.VMEM((tokens, width), low),
            pltpu.VMEM((width, block), low),
            pltpu.VMEM((block, width), low),
            pltpu.VMEM((tokens, block), jnp.int32),
            pltpu.VMEM((tokens, block), full),
            pltpu.VMEM((tokens, block), full),
            pltpu.VMEM((tokens, block), full),
            pltpu.VMEM((tokens, block), full),
            pltpu.VMEM((2 * tokens, block), low),
            pltpu.VMEM((CHUNKS, HALF, 2, SUB, wide), low),
            pltpu.VMEM((CHUNKS, HALF, 2, SUB, wide), low),
            pltpu.VMEM((CHUNKS, SUB, wide), low),
            pltpu.VMEM((CHUNKS, SUB, wide), low),
            pltpu.VMEM((CHUNKS, 5, SUB, wide), low),
            pltpu.VMEM((CHUNKS, HALF, 2, SUB, wide), low),
            pltpu.VMEM((1, width), full),
            pltpu.VMEM((HALF, 1, width), full),
            pltpu.VMEM((1, width), full),
            pltpu.VMEM((1, width), full),
            dma((3 + CHUNKS,)),
            dma((4,)),
            dma((CHUNKS, HALF)),
            dma((CHUNKS, HALF)),
            dma((CHUNKS + 1,)),
            dma((CHUNKS + 1,)),
            dma((CHUNKS, HALF)),
            dma((CHUNKS, HALF)),
            dma((HALF,)),
            dma((HALF,)),
            dma((1 + CHUNKS,)),
        ],
        compiler_params=pltpu.CompilerParams(
            collective_id=0, has_side_effects=True, vmem_limit_bytes=40 * 1024 * 1024
        ),
        name="exchange",
    )(
        activations, encoder, encoder_bias.reshape(1, block), decoder, decoder_bias.reshape(1, width), kept_mask,
        boundaries,
    )
    suffix = suffix.reshape(CHUNKS, 2 * tokens, wide)
    enc_grad, dec_grad, enc_bias_grad, dec_bias_grad = pl.pallas_call(
        grads_kernel,
        grid=(CHUNKS,),
        out_shape=[
            jax.ShapeDtypeStruct((width, block), low),
            jax.ShapeDtypeStruct((block, width), low),
            jax.ShapeDtypeStruct((1, block), full),
            jax.ShapeDtypeStruct((1, width), full),
        ],
        in_specs=[
            pl.BlockSpec((tokens, wide), lambda c: (0, c)),
            pl.BlockSpec((tokens, block), lambda c: (0, 0)),
            pl.BlockSpec((2 * tokens, block), lambda c: (0, 0)),
            pl.BlockSpec((1, 2 * tokens, wide), lambda c: (c, 0, 0)),
            pl.BlockSpec((1, block), lambda c: (0, 0)),
            pl.BlockSpec((1, width), lambda c: (0, 0)),
        ],
        out_specs=[
            pl.BlockSpec((wide, block), lambda c: (c, 0)),
            pl.BlockSpec((block, wide), lambda c: (0, c)),
            pl.BlockSpec((1, block), lambda c: (0, 0)),
            pl.BlockSpec((1, width), lambda c: (0, 0)),
        ],
        compiler_params=pltpu.CompilerParams(vmem_limit_bytes=32 * 1024 * 1024),
        name="grads",
    )(activations, pre, codes, suffix, enc_bias_grad, dec_bias_grad)
    return enc_grad, enc_bias_grad.reshape(block), dec_grad, dec_bias_grad.reshape(width)


def fits(mesh):
    return mesh.shape["lat"] == 2 * HALF and mesh.shape["wid"] == 2


def solution(mesh):
    placed = (
        P(None, "wid"),
        P("wid", "lat"),
        P("lat"),
        P("lat", "wid"),
        P("wid"),
        P(None, "lat"),
        P(),
    )
    return jax.shard_map(
        kernel_body if fits(mesh) else general_body,
        mesh=mesh,
        in_specs=placed,
        out_specs=(P("wid", "lat"), P("lat"), P("lat", "wid"), P("wid")),
        check_vma=False,
    )
```

```python
import functools

import jax
import jax.numpy as jnp
from jax import lax
from jax.experimental import pallas as pl
from jax.experimental.pallas import tpu as pltpu
from jax.sharding import PartitionSpec as P

GROUPS = 8
HALF = 8
SUB = 16
LANES = 128
STEPS = 2
MESH = pl.DeviceIdType.MESH


def prefix(part, axis, combine, identity, reverse):
    count = lax.axis_size(axis)
    place = lax.axis_index(axis)
    ahead = count - 1 - place if reverse else place
    gathered = lax.all_gather(part, axis)
    state = jnp.zeros_like(part) + jnp.asarray(identity, part.dtype)

    def one(step, state):
        source = count - 1 - step if reverse else step
        return combine(state, lax.dynamic_index_in_dim(gathered, source, 0, False))

    return lax.fori_loop(0, ahead, one, state)


def add_terms(earlier, later):
    return earlier + later


def general_body(activations, encoder, encoder_bias, decoder, decoder_bias, kept_mask, boundaries):
    latent_width = encoder.shape[1]
    first_latent = lax.axis_index("lat") * latent_width
    latent_ids = first_latent + jnp.arange(latent_width, dtype=jnp.int32)
    kept_float = kept_mask.astype(jnp.float32)
    encoder_part = jnp.dot(activations, encoder, preferred_element_type=jnp.float32)
    preacts = lax.psum(encoder_part, "wid") + encoder_bias
    codes = (kept_float * preacts).astype(jnp.bfloat16)
    inside_rows = (boundaries > first_latent) & (boundaries <= first_latent + latent_width)
    holds_cut = jnp.any(inside_rows)
    cut_point = jnp.sum(jnp.where(inside_rows, boundaries, 0))
    below_cut = latent_ids < cut_point
    zero_code = jnp.zeros((), jnp.bfloat16)
    masked_codes = jnp.stack(
        [
            jnp.where(below_cut[None, :], codes, zero_code),
            jnp.where(below_cut[None, :], zero_code, codes),
        ]
    )
    decoded_pieces = jnp.einsum(
        "sbj,jd->sbd", masked_codes, decoder, preferred_element_type=jnp.float32
    )
    local_total = decoded_pieces[0] + decoded_pieces[1]
    zero_rows = jnp.zeros_like(local_total)
    prefix_sum = prefix(local_total, "lat", add_terms, zero_rows, False)
    target_rows = activations.astype(jnp.float32)
    scaled_error = jnp.where(
        holds_cut, (decoder_bias + prefix_sum + decoded_pieces[0] - target_rows) / GROUPS, 0.0
    )
    suffix_sum = prefix(scaled_error, "lat", add_terms, zero_rows, True)
    below_suffix = suffix_sum + scaled_error
    suffix_pair = jnp.stack([below_suffix, suffix_sum]).astype(jnp.bfloat16)
    back_grads = jnp.einsum("sbd,jd->sbj", suffix_pair, decoder, preferred_element_type=jnp.float32)
    partial_grads = jnp.where(below_cut[None, :], back_grads[0], back_grads[1])
    coded_grads = lax.psum(partial_grads, "wid")
    pre_grads = kept_float * coded_grads
    encoder_bias_grad = jnp.sum(pre_grads, axis=0)
    pre_low = pre_grads.astype(jnp.bfloat16)
    encoder_grad = lax.dot_general(
        activations, pre_low, (((0,), (0,)), ((), ())), preferred_element_type=jnp.float32
    ).astype(jnp.bfloat16)
    decoder_grad = jnp.einsum(
        "sbj,sbd->jd", masked_codes, suffix_pair, preferred_element_type=jnp.float32
    ).astype(jnp.bfloat16)
    decoder_bias_grad = lax.psum(jnp.sum(scaled_error, axis=0), "lat")
    return (encoder_grad, encoder_bias_grad, decoder_grad, decoder_bias_grad)


def column_chunks(width):
    tiles = width // LANES
    widths = []
    while tiles > 0:
        widths.append(min(2 if not widths else 4, tiles))
        tiles -= widths[-1]
    ends = [LANES * sum(widths[: k + 1]) for k in range(len(widths))]
    return [slice(end - LANES * count, end) for end, count in zip(ends, widths)]


def reduce_pieces(pieces, span):
    def piece(source, which):
        return pieces[source, which, :, span].astype(jnp.float32)

    upper = [piece(2 * k, 1) + piece(2 * k + 1, 1) for k in range(4)]
    lower = [piece(2 * k, 0) for k in range(4)]
    segments = [upper[k] + lower[k + 1] for k in range(3)] + [upper[3]]
    return lower[0], segments


def exchange_kernel(
    act_hbm, enc_hbm, enc_bias_hbm, dec_hbm, dec_bias_hbm, mask_hbm, bounds,
    codes_out, suffix_out, pre_out, enc_bias_out, dec_bias_out,
    act, enc, enc_bias, dec, dec_bias, mask, part, part_in, grad, grad_in, codes,
    pieces_out, pieces, cross_out, cross_in, tails, suffix,
    row_out, rows, final_out, final_in,
    load_sems, wid_sems, a_send, a_recv, x_send, x_recv, b_send, b_recv, r_send, r_recv, store_sems,
):
    lat = lax.axis_index("lat")
    wid = lax.axis_index("wid")
    half = lat // HALF
    place = lat % HALF
    even = place % 2 == 0
    odd = place % 2 == 1
    width = act.shape[1]
    spans = column_chunks(width)
    chunks = len(spans)
    views = [pl.ds(span.start, span.stop - span.start) for span in spans]
    block = dec.shape[0]
    other_core = {"lat": lat, "wid": 1 - wid}
    other_half = {"lat": (lat + HALF) % (2 * HALF), "wid": wid}

    def peer(step):
        return (place + step) % HALF

    def source(step):
        return (place + HALF - step) % HALF

    def device(position):
        return {"lat": half * HALF + position, "wid": wid}

    def remote(src, dst, send, recv, target):
        return pltpu.make_async_remote_copy(
            src_ref=src, dst_ref=dst, send_sem=send, recv_sem=recv, device_id=target, device_id_type=MESH
        )

    barrier = pltpu.get_barrier_semaphore()
    for step in range(1, HALF):
        pl.semaphore_signal(barrier, inc=1, device_id=device(peer(step)), device_id_type=MESH)
    pl.semaphore_signal(barrier, inc=1, device_id=other_core, device_id_type=MESH)
    pl.semaphore_signal(barrier, inc=1, device_id=other_half, device_id_type=MESH)

    load_act = pltpu.make_async_copy(act_hbm, act, load_sems.at[0])
    load_act.start()
    load_enc = []
    for c in range(2):
        rows_of = pl.ds(c * (width // 2), width // 2)
        load_enc.append(pltpu.make_async_copy(enc_hbm.at[rows_of], enc.at[rows_of], load_sems.at[1 + c]))
        load_enc[-1].start()
    load_mask = pltpu.make_async_copy(mask_hbm, mask, load_sems.at[3])
    load_mask.start()
    load_enc_bias = pltpu.make_async_copy(enc_bias_hbm, enc_bias.at[0], load_sems.at[4])
    load_enc_bias.start()
    load_dec = pltpu.make_async_copy(dec_hbm, dec, load_sems.at[5])
    load_dec.start()
    load_dec_bias = pltpu.make_async_copy(dec_bias_hbm, dec_bias.at[0], load_sems.at[6])
    load_dec_bias.start()

    @pl.when(odd)
    def _():
        for r in range(HALF):
            suffix[r, 0] = jnp.zeros((SUB, width), jnp.bfloat16)

    load_act.wait()
    total = None
    for c in range(2):
        load_enc[c].wait()
        deep = slice(c * (width // 2), (c + 1) * (width // 2))
        term = jnp.dot(act[:, deep], enc[deep, :], preferred_element_type=jnp.float32)
        total = term if total is None else total + term
    part[...] = total
    pl.semaphore_wait(barrier, HALF + 1)
    swap = remote(part, part_in, wid_sems.at[0], wid_sems.at[1], other_core)
    swap.start()

    first = lat * block
    cut = jnp.int32(0)
    for k in range(GROUPS - 1):
        bound = bounds[k]
        cut = cut + jnp.where((bound > first) & (bound <= first + block), bound, 0)
    tokens = act.shape[0]
    below = (lax.broadcasted_iota(jnp.int32, (tokens, block), 1) + first) < cut
    load_mask.wait()
    load_enc_bias.wait()
    load_dec_bias.wait()
    kept = mask[...].astype(jnp.float32)
    load_dec.wait()
    swap.wait()
    full = kept * ((part[...] + part_in[...]) + enc_bias[...])
    low = jnp.where(below, full, 0.0).astype(jnp.bfloat16)
    high = jnp.where(below, 0.0, full).astype(jnp.bfloat16)
    for r in range(HALF):
        codes[2 * SUB * r : 2 * SUB * r + SUB, :] = low[SUB * r : SUB * (r + 1), :]
        codes[2 * SUB * r + SUB : 2 * SUB * (r + 1), :] = high[SUB * r : SUB * (r + 1), :]
    store_codes = pltpu.make_async_copy(codes, codes_out, store_sems.at[0])
    store_codes.start()

    def send_pieces(c, step, both):
        target = peer(step)
        if both:
            src, dst = pieces_out.at[target, :, :, views[c]], pieces.at[place, :, :, views[c]]
        else:
            src, dst = pieces_out.at[target, 1, :, views[c]], pieces.at[place, 1, :, views[c]]
        return remote(src, dst, a_send.at[c, step], a_recv.at[c, place], device(target))

    def wait_pieces(c, step):
        origin = source(step)

        @pl.when(origin % 2 == 0)
        def _():
            ref = pieces.at[origin, :, :, views[c]]
            remote(ref, ref, a_send.at[c, step], a_recv.at[c, origin], device(origin)).wait_recv()

        @pl.when(origin % 2 == 1)
        def _():
            ref = pieces.at[origin, 1, :, views[c]]
            remote(ref, ref, a_send.at[c, step], a_recv.at[c, origin], device(origin)).wait_recv()

    for c in range(chunks):
        span = spans[c]
        made = jnp.dot(codes[...], dec[:, span], preferred_element_type=jnp.float32)
        pieces_out[:, :, :, span] = made.astype(jnp.bfloat16).reshape(HALF, 2, SUB, span.stop - span.start)

        @pl.when(even)
        def _():
            for step in range(1, HALF):
                send_pieces(c, step, True).start()

        @pl.when(odd)
        def _():
            for step in range(1, HALF):
                send_pieces(c, step, False).start()

        pieces[place, :, :, span] = pieces_out[place, :, :, span]

    crossing = []
    for c in range(chunks):
        for step in range(1, HALF):
            wait_pieces(c, step)
        low0, seg = reduce_pieces(pieces, spans[c])
        plain = ((low0 + seg[0]) + seg[1]) + (seg[2] + seg[3])
        weighted = ((5.0 * low0 + 4.0 * seg[0]) + 3.0 * seg[1]) + (2.0 * seg[2] + seg[3])
        cross_out[:, spans[c]] = jnp.where(half == 0, plain, weighted).astype(jnp.bfloat16)
        crossing.append(remote(cross_out.at[:, views[c]], cross_in.at[:, views[c]], x_send.at[c], x_recv.at[c], other_half))
        crossing[-1].start()

    def send_suffix(c, step, both):
        target = peer(step)
        if both:
            src, dst = tails.at[pl.ds(target // 2, 2), :, views[c]], suffix.at[place, :, :, views[c]]
        else:
            src, dst = tails.at[target // 2 + 1, :, views[c]], suffix.at[place, 1, :, views[c]]
        return remote(src, dst, b_send.at[c, step], b_recv.at[c, place], device(target))

    later = half.astype(jnp.float32)
    own_rows = pl.ds(pl.multiple_of(place * SUB, SUB), SUB)
    for c in range(chunks):
        span = spans[c]
        low0, seg = reduce_pieces(pieces, spans[c])
        crossing[c].wait_recv()
        got = cross_in[:, span].astype(jnp.float32)
        base = dec_bias[:, span] - act[own_rows, span].astype(jnp.float32)
        before = base + later * (got + low0)
        errors = []
        running = before
        for k in range(4):
            running = running + seg[k]
            errors.append(running)
        tail = jnp.where(half == 0, 5.0 * errors[3] + got, errors[3])
        scaled = [tail]
        for k in (2, 1, 0):
            tail = tail + errors[k]
            scaled.append(tail)
        scaled.append(tail + before)
        for k in range(5):
            tails[k, :, span] = (scaled[4 - k] / GROUPS).astype(jnp.bfloat16)
        row_out[:, span] = jnp.sum(scaled[3] / GROUPS, axis=0, keepdims=True)
        for step in range(1, HALF):

            @pl.when(peer(step) % 2 == 0)
            def _():
                send_suffix(c, step, True).start()

            @pl.when(peer(step) % 2 == 1)
            def _():
                send_suffix(c, step, False).start()

        suffix[place, :, :, span] = tails[pl.ds(place // 2, 2), :, span]

    def row_copy(step):
        return remote(row_out, rows.at[place], r_send.at[step], r_recv.at[place], device(peer(step)))

    for step in range(1, HALF):
        row_copy(step).start()
    rows[place] = row_out[...]

    back = None
    stores = []
    for c in range(chunks):

        @pl.when(even)
        def _():
            for step in range(1, HALF):
                origin = source(step)
                ref = suffix.at[origin, :, :, views[c]]
                remote(ref, ref, b_send.at[c, step], b_recv.at[c, origin], device(origin)).wait_recv()

        @pl.when(odd)
        def _():
            for step in range(1, HALF):
                origin = source(step)
                ref = suffix.at[origin, 1, :, views[c]]
                remote(ref, ref, b_send.at[c, step], b_recv.at[c, origin], device(origin)).wait_recv()

        span = spans[c]
        there = suffix_out.at[:, :, :, views[c]]
        stores.append(pltpu.make_async_copy(suffix.at[:, :, :, views[c]], there, store_sems.at[1 + c]))
        stores[-1].start()
        term = lax.dot_general(
            suffix[:, :, :, span].reshape(2 * tokens, span.stop - span.start), dec[:, span],
            (((1,), (1,)), ((), ())), preferred_element_type=jnp.float32,
        )
        back = term if back is None else back + term
    pair = back.reshape(HALF, 2, SUB, block)
    below_parts = below.astype(jnp.float32).reshape(HALF, SUB, block) > 0.5
    grad[...] = jnp.where(below_parts, pair[:, 0], pair[:, 1]).reshape(tokens, block)
    swap_back = remote(grad, grad_in, wid_sems.at[2], wid_sems.at[3], other_core)
    swap_back.start()

    for step in range(1, HALF):
        origin = source(step)
        remote(row_out, rows.at[origin], r_send.at[step], r_recv.at[origin], device(origin)).wait_recv()
    summed = rows[0]
    for r in range(1, HALF):
        summed = summed + rows[r]
    final_out[...] = summed
    finish = remote(final_out, final_in, x_send.at[chunks], x_recv.at[chunks], other_half)
    finish.start()

    swap_back.wait()
    pre = kept * (grad[...] + grad_in[...])
    enc_bias_out[...] = jnp.sum(pre, axis=0, keepdims=True)
    pre_out[...] = pre.astype(jnp.bfloat16)

    for c in range(chunks):
        crossing[c].wait_send()

        @pl.when(even)
        def _():
            for step in range(1, HALF):
                send_pieces(c, step, True).wait_send()

        @pl.when(odd)
        def _():
            for step in range(1, HALF):
                send_pieces(c, step, False).wait_send()

        for step in range(1, HALF):

            @pl.when(peer(step) % 2 == 0)
            def _():
                send_suffix(c, step, True).wait_send()

            @pl.when(peer(step) % 2 == 1)
            def _():
                send_suffix(c, step, False).wait_send()

    for step in range(1, HALF):
        row_copy(step).wait_send()
    finish.wait()
    dec_bias_out[...] = jnp.where(half == 0, final_out[...], final_in[...])
    store_codes.wait()
    for store in stores:
        store.wait()


def grads_kernel(act, pre, codes, suffix, enc_bias_in, dec_bias_in, enc_grad, dec_grad, enc_bias_out, dec_bias_out):
    contract_rows = (((0,), (0,)), ((), ()))
    enc_grad[...] = lax.dot_general(act[...], pre[...], contract_rows, preferred_element_type=jnp.float32).astype(
        jnp.bfloat16
    )
    dec_grad[...] = lax.dot_general(
        codes[...], suffix[...], contract_rows, preferred_element_type=jnp.float32
    ).astype(jnp.bfloat16)
    enc_bias_out[...] = enc_bias_in[0]
    dec_bias_out[...] = dec_bias_in[0]


def kernel_body(activations, encoder, encoder_bias, decoder, decoder_bias, kept_mask, boundaries):
    tokens, width = activations.shape
    block = encoder.shape[1]
    chunks = len(column_chunks(width))
    wide = width // STEPS
    low, full = jnp.bfloat16, jnp.float32
    hbm = pl.BlockSpec(memory_space=pltpu.HBM)
    vmem = pl.BlockSpec(memory_space=pltpu.VMEM)
    smem = pl.BlockSpec(memory_space=pltpu.SMEM)
    dma = pltpu.SemaphoreType.DMA
    codes, suffix, pre, enc_bias_grad, dec_bias_grad = pl.pallas_call(
        exchange_kernel,
        out_shape=[
            jax.ShapeDtypeStruct((2 * tokens, block), low),
            jax.ShapeDtypeStruct((HALF, 2, SUB, width), low),
            jax.ShapeDtypeStruct((tokens, block), low),
            jax.ShapeDtypeStruct((1, block), full),
            jax.ShapeDtypeStruct((1, width), full),
        ],
        in_specs=[hbm, hbm, hbm, hbm, hbm, hbm, smem],
        out_specs=[hbm, hbm, vmem, vmem, vmem],
        scratch_shapes=[
            pltpu.VMEM((tokens, width), low),
            pltpu.VMEM((width, block), low),
            pltpu.VMEM((1, block), full),
            pltpu.VMEM((block, width), low),
            pltpu.VMEM((1, width), full),
            pltpu.VMEM((tokens, block), jnp.int32),
            pltpu.VMEM((tokens, block), full),
            pltpu.VMEM((tokens, block), full),
            pltpu.VMEM((tokens, block), full),
            pltpu.VMEM((tokens, block), full),
            pltpu.VMEM((2 * tokens, block), low),
            pltpu.VMEM((HALF, 2, SUB, width), low),
            pltpu.VMEM((HALF, 2, SUB, width), low),
            pltpu.VMEM((SUB, width), low),
            pltpu.VMEM((SUB, width), low),
            pltpu.VMEM((5, SUB, width), low),
            pltpu.VMEM((HALF, 2, SUB, width), low),
            pltpu.VMEM((1, width), full),
            pltpu.VMEM((HALF, 1, width), full),
            pltpu.VMEM((1, width), full),
            pltpu.VMEM((1, width), full),
            dma((7,)),
            dma((4,)),
            dma((chunks, HALF)),
            dma((chunks, HALF)),
            dma((chunks + 1,)),
            dma((chunks + 1,)),
            dma((chunks, HALF)),
            dma((chunks, HALF)),
            dma((HALF,)),
            dma((HALF,)),
            dma((1 + chunks,)),
        ],
        compiler_params=pltpu.CompilerParams(
            collective_id=0, has_side_effects=True, vmem_limit_bytes=60 * 1024 * 1024
        ),
        name="exchange",
    )(
        activations, encoder, encoder_bias, decoder, decoder_bias, kept_mask, boundaries,
    )
    suffix = suffix.reshape(2 * tokens, width)
    enc_grad, dec_grad, enc_bias_grad, dec_bias_grad = pl.pallas_call(
        grads_kernel,
        grid=(STEPS,),
        out_shape=[
            jax.ShapeDtypeStruct((width, block), low),
            jax.ShapeDtypeStruct((block, width), low),
            jax.ShapeDtypeStruct((block,), full),
            jax.ShapeDtypeStruct((width,), full),
        ],
        in_specs=[
            pl.BlockSpec((tokens, wide), lambda c: (0, c)),
            pl.BlockSpec((tokens, block), lambda c: (0, 0)),
            pl.BlockSpec((2 * tokens, block), lambda c: (0, 0)),
            pl.BlockSpec((2 * tokens, wide), lambda c: (0, c)),
            pl.BlockSpec((1, block), lambda c: (0, 0)),
            pl.BlockSpec((1, width), lambda c: (0, 0)),
        ],
        out_specs=[
            pl.BlockSpec((wide, block), lambda c: (c, 0)),
            pl.BlockSpec((block, wide), lambda c: (0, c)),
            pl.BlockSpec((block,), lambda c: (0,)),
            pl.BlockSpec((width,), lambda c: (0,)),
        ],
        compiler_params=pltpu.CompilerParams(vmem_limit_bytes=60 * 1024 * 1024),
        name="grads",
    )(activations, pre, codes, suffix, enc_bias_grad, dec_bias_grad)
    return enc_grad, enc_bias_grad, dec_grad, dec_bias_grad


def fits(mesh):
    return mesh.shape["lat"] == 2 * HALF and mesh.shape["wid"] == 2


def solution(mesh):
    placed = (
        P(None, "wid"),
        P("wid", "lat"),
        P("lat"),
        P("lat", "wid"),
        P("wid"),
        P(None, "lat"),
        P(),
    )
    return jax.shard_map(
        kernel_body if fits(mesh) else general_body,
        mesh=mesh,
        in_specs=placed,
        out_specs=(P("wid", "lat"), P("lat"), P("lat", "wid"), P("wid")),
        check_vma=False,
    )
```

```python
import functools

import jax
import jax.numpy as jnp
from jax import lax
from jax.experimental import pallas as pl
from jax.experimental.pallas import tpu as pltpu
from jax.sharding import PartitionSpec as P

GROUPS = 8
HALF = 8
SUB = 16
LANES = 128
STEPS = 7
MESH = pl.DeviceIdType.MESH


def prefix(part, axis, combine, identity, reverse):
    count = lax.axis_size(axis)
    place = lax.axis_index(axis)
    ahead = count - 1 - place if reverse else place
    gathered = lax.all_gather(part, axis)
    state = jnp.zeros_like(part) + jnp.asarray(identity, part.dtype)

    def one(step, state):
        source = count - 1 - step if reverse else step
        return combine(state, lax.dynamic_index_in_dim(gathered, source, 0, False))

    return lax.fori_loop(0, ahead, one, state)


def add_terms(earlier, later):
    return earlier + later


def general_body(activations, encoder, encoder_bias, decoder, decoder_bias, kept_mask, boundaries):
    latent_width = encoder.shape[1]
    first_latent = lax.axis_index("lat") * latent_width
    latent_ids = first_latent + jnp.arange(latent_width, dtype=jnp.int32)
    kept_float = kept_mask.astype(jnp.float32)
    encoder_part = jnp.dot(activations, encoder, preferred_element_type=jnp.float32)
    preacts = lax.psum(encoder_part, "wid") + encoder_bias
    codes = (kept_float * preacts).astype(jnp.bfloat16)
    inside_rows = (boundaries > first_latent) & (boundaries <= first_latent + latent_width)
    holds_cut = jnp.any(inside_rows)
    cut_point = jnp.sum(jnp.where(inside_rows, boundaries, 0))
    below_cut = latent_ids < cut_point
    zero_code = jnp.zeros((), jnp.bfloat16)
    masked_codes = jnp.stack(
        [
            jnp.where(below_cut[None, :], codes, zero_code),
            jnp.where(below_cut[None, :], zero_code, codes),
        ]
    )
    decoded_pieces = jnp.einsum(
        "sbj,jd->sbd", masked_codes, decoder, preferred_element_type=jnp.float32
    )
    local_total = decoded_pieces[0] + decoded_pieces[1]
    zero_rows = jnp.zeros_like(local_total)
    prefix_sum = prefix(local_total, "lat", add_terms, zero_rows, False)
    target_rows = activations.astype(jnp.float32)
    scaled_error = jnp.where(
        holds_cut, (decoder_bias + prefix_sum + decoded_pieces[0] - target_rows) / GROUPS, 0.0
    )
    suffix_sum = prefix(scaled_error, "lat", add_terms, zero_rows, True)
    below_suffix = suffix_sum + scaled_error
    suffix_pair = jnp.stack([below_suffix, suffix_sum]).astype(jnp.bfloat16)
    back_grads = jnp.einsum("sbd,jd->sbj", suffix_pair, decoder, preferred_element_type=jnp.float32)
    partial_grads = jnp.where(below_cut[None, :], back_grads[0], back_grads[1])
    coded_grads = lax.psum(partial_grads, "wid")
    pre_grads = kept_float * coded_grads
    encoder_bias_grad = jnp.sum(pre_grads, axis=0)
    pre_low = pre_grads.astype(jnp.bfloat16)
    encoder_grad = lax.dot_general(
        activations, pre_low, (((0,), (0,)), ((), ())), preferred_element_type=jnp.float32
    ).astype(jnp.bfloat16)
    decoder_grad = jnp.einsum(
        "sbj,sbd->jd", masked_codes, suffix_pair, preferred_element_type=jnp.float32
    ).astype(jnp.bfloat16)
    decoder_bias_grad = lax.psum(jnp.sum(scaled_error, axis=0), "lat")
    return (encoder_grad, encoder_bias_grad, decoder_grad, decoder_bias_grad)


def column_chunks(width):
    tiles = width // LANES
    widths = []
    while tiles > 0:
        widths.append(min(4 if len(widths) in (1, 2) else 2, tiles))
        tiles -= widths[-1]
    ends = [LANES * sum(widths[: k + 1]) for k in range(len(widths))]
    return [slice(end - LANES * count, end) for end, count in zip(ends, widths)]


def reduce_pieces(pieces, span):
    def piece(source, which):
        return pieces[source, which, :, span].astype(jnp.float32)

    upper = [piece(2 * k, 1) + piece(2 * k + 1, 1) for k in range(4)]
    lower = [piece(2 * k, 0) for k in range(4)]
    segments = [upper[k] + lower[k + 1] for k in range(3)] + [upper[3]]
    return lower[0], segments


def exchange_kernel(
    act_hbm, enc_hbm, enc_bias_hbm, dec_hbm, dec_bias_hbm, mask_hbm, bounds,
    codes_out, suffix_out, pre_out, enc_bias_out, dec_bias_out,
    act, enc, enc_bias, dec, dec_bias, mask, part, part_in, grad, grad_in, codes,
    pieces_out, pieces, cross_out, cross_in, tails, suffix,
    row_out, rows, final_out, final_in,
    load_sems, wid_sems, a_send, a_recv, x_send, x_recv, b_send, b_recv, r_send, r_recv, store_sems,
):
    lat = lax.axis_index("lat")
    wid = lax.axis_index("wid")
    half = lat // HALF
    place = lat % HALF
    even = place % 2 == 0
    odd = place % 2 == 1
    width = act.shape[1]
    spans = column_chunks(width)
    chunks = len(spans)
    views = [pl.ds(span.start, span.stop - span.start) for span in spans]
    block = dec.shape[0]
    other_core = {"lat": lat, "wid": 1 - wid}
    other_half = {"lat": (lat + HALF) % (2 * HALF), "wid": wid}

    def peer(step):
        return (place + step) % HALF

    def source(step):
        return (place + HALF - step) % HALF

    def device(position):
        return {"lat": half * HALF + position, "wid": wid}

    def remote(src, dst, send, recv, target):
        return pltpu.make_async_remote_copy(
            src_ref=src, dst_ref=dst, send_sem=send, recv_sem=recv, device_id=target, device_id_type=MESH
        )

    barrier = pltpu.get_barrier_semaphore()
    for step in range(1, HALF):
        pl.semaphore_signal(barrier, inc=1, device_id=device(peer(step)), device_id_type=MESH)
    pl.semaphore_signal(barrier, inc=1, device_id=other_core, device_id_type=MESH)
    pl.semaphore_signal(barrier, inc=1, device_id=other_half, device_id_type=MESH)

    load_act = pltpu.make_async_copy(act_hbm, act, load_sems.at[0])
    load_act.start()
    load_enc = []
    for c in range(2):
        rows_of = pl.ds(c * (width // 2), width // 2)
        load_enc.append(pltpu.make_async_copy(enc_hbm.at[rows_of], enc.at[rows_of], load_sems.at[1 + c]))
        load_enc[-1].start()
    load_mask = pltpu.make_async_copy(mask_hbm, mask, load_sems.at[3])
    load_mask.start()
    load_enc_bias = pltpu.make_async_copy(enc_bias_hbm, enc_bias.at[0], load_sems.at[4])
    load_enc_bias.start()
    load_dec = pltpu.make_async_copy(dec_hbm, dec, load_sems.at[5])
    load_dec.start()
    load_dec_bias = pltpu.make_async_copy(dec_bias_hbm, dec_bias.at[0], load_sems.at[6])
    load_dec_bias.start()

    @pl.when(odd)
    def _():
        for r in range(HALF):
            suffix[r, 0] = jnp.zeros((SUB, width), jnp.bfloat16)

    load_act.wait()
    total = None
    for c in range(2):
        load_enc[c].wait()
        deep = slice(c * (width // 2), (c + 1) * (width // 2))
        term = jnp.dot(act[:, deep], enc[deep, :], preferred_element_type=jnp.float32)
        total = term if total is None else total + term
    part[...] = total
    pl.semaphore_wait(barrier, HALF + 1)
    swap = remote(part, part_in, wid_sems.at[0], wid_sems.at[1], other_core)
    swap.start()

    first = lat * block
    cut = jnp.int32(0)
    for k in range(GROUPS - 1):
        bound = bounds[k]
        cut = cut + jnp.where((bound > first) & (bound <= first + block), bound, 0)
    tokens = act.shape[0]
    below = (lax.broadcasted_iota(jnp.int32, (tokens, block), 1) + first) < cut
    load_mask.wait()
    load_enc_bias.wait()
    load_dec_bias.wait()
    kept = mask[...].astype(jnp.float32)
    load_dec.wait()
    swap.wait()
    full = kept * ((part[...] + part_in[...]) + enc_bias[...])
    low = jnp.where(below, full, 0.0).astype(jnp.bfloat16)
    high = jnp.where(below, 0.0, full).astype(jnp.bfloat16)
    for r in range(HALF):
        codes[2 * SUB * r : 2 * SUB * r + SUB, :] = low[SUB * r : SUB * (r + 1), :]
        codes[2 * SUB * r + SUB : 2 * SUB * (r + 1), :] = high[SUB * r : SUB * (r + 1), :]
    store_codes = pltpu.make_async_copy(codes, codes_out, store_sems.at[0])
    store_codes.start()

    def send_pieces(c, step, both):
        target = peer(step)
        if both:
            src, dst = pieces_out.at[target, :, :, views[c]], pieces.at[place, :, :, views[c]]
        else:
            src, dst = pieces_out.at[target, 1, :, views[c]], pieces.at[place, 1, :, views[c]]
        return remote(src, dst, a_send.at[c, step], a_recv.at[c, place], device(target))

    def wait_pieces(c, step):
        origin = source(step)

        @pl.when(origin % 2 == 0)
        def _():
            ref = pieces.at[origin, :, :, views[c]]
            remote(ref, ref, a_send.at[c, step], a_recv.at[c, origin], device(origin)).wait_recv()

        @pl.when(origin % 2 == 1)
        def _():
            ref = pieces.at[origin, 1, :, views[c]]
            remote(ref, ref, a_send.at[c, step], a_recv.at[c, origin], device(origin)).wait_recv()

    for c in range(chunks):
        span = spans[c]
        made = jnp.dot(codes[...], dec[:, span], preferred_element_type=jnp.float32)
        pieces_out[:, :, :, span] = made.astype(jnp.bfloat16).reshape(HALF, 2, SUB, span.stop - span.start)

        @pl.when(even)
        def _():
            for step in range(1, HALF):
                send_pieces(c, step, True).start()

        @pl.when(odd)
        def _():
            for step in range(1, HALF):
                send_pieces(c, step, False).start()

        pieces[place, :, :, span] = pieces_out[place, :, :, span]

    crossing = []

    def cross(c):
        for step in range(1, HALF):
            wait_pieces(c, step)
        low0, seg = reduce_pieces(pieces, spans[c])
        plain = ((low0 + seg[0]) + seg[1]) + (seg[2] + seg[3])
        weighted = ((5.0 * low0 + 4.0 * seg[0]) + 3.0 * seg[1]) + (2.0 * seg[2] + seg[3])
        cross_out[:, spans[c]] = jnp.where(half == 0, plain, weighted).astype(jnp.bfloat16)
        crossing.append(
            remote(cross_out.at[:, views[c]], cross_in.at[:, views[c]], x_send.at[c], x_recv.at[c], other_half)
        )
        crossing[-1].start()

    def send_suffix(c, step, both):
        target = peer(step)
        if both:
            src, dst = tails.at[pl.ds(target // 2, 2), :, views[c]], suffix.at[place, :, :, views[c]]
        else:
            src, dst = tails.at[target // 2 + 1, :, views[c]], suffix.at[place, 1, :, views[c]]
        return remote(src, dst, b_send.at[c, step], b_recv.at[c, place], device(target))

    later = half.astype(jnp.float32)
    own_rows = pl.ds(pl.multiple_of(place * SUB, SUB), SUB)
    def finalize(c):
        span = spans[c]
        low0, seg = reduce_pieces(pieces, spans[c])
        crossing[c].wait_recv()
        got = cross_in[:, span].astype(jnp.float32)
        base = dec_bias[:, span] - act[own_rows, span].astype(jnp.float32)
        before = base + later * (got + low0)
        errors = []
        running = before
        for k in range(4):
            running = running + seg[k]
            errors.append(running)
        tail = jnp.where(half == 0, 5.0 * errors[3] + got, errors[3])
        scaled = [tail]
        for k in (2, 1, 0):
            tail = tail + errors[k]
            scaled.append(tail)
        scaled.append(tail + before)
        for k in range(5):
            tails[k, :, span] = (scaled[4 - k] / GROUPS).astype(jnp.bfloat16)
        row_out[:, span] = jnp.sum(scaled[3] / GROUPS, axis=0, keepdims=True)
        for step in range(1, HALF):

            @pl.when(peer(step) % 2 == 0)
            def _():
                send_suffix(c, step, True).start()

            @pl.when(peer(step) % 2 == 1)
            def _():
                send_suffix(c, step, False).start()

        suffix[place, :, :, span] = tails[pl.ds(place // 2, 2), :, span]

    for c in range(chunks + 1):
        if c < chunks:
            cross(c)
        if c > 0:
            finalize(c - 1)

    def row_copy(step):
        return remote(row_out, rows.at[place], r_send.at[step], r_recv.at[place], device(peer(step)))

    for step in range(1, HALF):
        row_copy(step).start()
    rows[place] = row_out[...]

    back = None
    stores = []
    for c in range(chunks):

        @pl.when(even)
        def _():
            for step in range(1, HALF):
                origin = source(step)
                ref = suffix.at[origin, :, :, views[c]]
                remote(ref, ref, b_send.at[c, step], b_recv.at[c, origin], device(origin)).wait_recv()

        @pl.when(odd)
        def _():
            for step in range(1, HALF):
                origin = source(step)
                ref = suffix.at[origin, 1, :, views[c]]
                remote(ref, ref, b_send.at[c, step], b_recv.at[c, origin], device(origin)).wait_recv()

        span = spans[c]
        there = suffix_out.at[:, :, :, views[c]]
        stores.append(pltpu.make_async_copy(suffix.at[:, :, :, views[c]], there, store_sems.at[1 + c]))
        stores[-1].start()
        term = lax.dot_general(
            suffix[:, :, :, span].reshape(2 * tokens, span.stop - span.start), dec[:, span],
            (((1,), (1,)), ((), ())), preferred_element_type=jnp.float32,
        )
        back = term if back is None else back + term
    pair = back.reshape(HALF, 2, SUB, block)
    below_parts = below.astype(jnp.float32).reshape(HALF, SUB, block) > 0.5
    grad[...] = jnp.where(below_parts, pair[:, 0], pair[:, 1]).reshape(tokens, block)
    swap_back = remote(grad, grad_in, wid_sems.at[2], wid_sems.at[3], other_core)
    swap_back.start()

    for step in range(1, HALF):
        origin = source(step)
        remote(row_out, rows.at[origin], r_send.at[step], r_recv.at[origin], device(origin)).wait_recv()
    summed = rows[0]
    for r in range(1, HALF):
        summed = summed + rows[r]
    final_out[...] = summed
    finish = remote(final_out, final_in, x_send.at[chunks], x_recv.at[chunks], other_half)
    finish.start()

    swap_back.wait()
    pre = kept * (grad[...] + grad_in[...])
    enc_bias_out[...] = jnp.sum(pre, axis=0, keepdims=True)
    pre_out[...] = pre.astype(jnp.bfloat16)

    for c in range(chunks):
        crossing[c].wait_send()

        @pl.when(even)
        def _():
            for step in range(1, HALF):
                send_pieces(c, step, True).wait_send()

        @pl.when(odd)
        def _():
            for step in range(1, HALF):
                send_pieces(c, step, False).wait_send()

        for step in range(1, HALF):

            @pl.when(peer(step) % 2 == 0)
            def _():
                send_suffix(c, step, True).wait_send()

            @pl.when(peer(step) % 2 == 1)
            def _():
                send_suffix(c, step, False).wait_send()

    for step in range(1, HALF):
        row_copy(step).wait_send()
    finish.wait()
    dec_bias_out[...] = jnp.where(half == 0, final_out[...], final_in[...])
    store_codes.wait()
    for store in stores:
        store.wait()


def grads_kernel(act, pre, codes, suffix, enc_bias_in, dec_bias_in, enc_grad, dec_grad, enc_bias_out, dec_bias_out):
    contract_rows = (((0,), (0,)), ((), ()))
    enc_grad[...] = lax.dot_general(act[...], pre[...], contract_rows, preferred_element_type=jnp.float32).astype(
        jnp.bfloat16
    )
    dec_grad[...] = lax.dot_general(
        codes[...], suffix[...], contract_rows, preferred_element_type=jnp.float32
    ).astype(jnp.bfloat16)
    enc_bias_out[...] = enc_bias_in[0]
    dec_bias_out[...] = dec_bias_in[0]


def kernel_body(activations, encoder, encoder_bias, decoder, decoder_bias, kept_mask, boundaries):
    tokens, width = activations.shape
    block = encoder.shape[1]
    chunks = len(column_chunks(width))
    wide = width // STEPS
    low, full = jnp.bfloat16, jnp.float32
    hbm = pl.BlockSpec(memory_space=pltpu.HBM)
    vmem = pl.BlockSpec(memory_space=pltpu.VMEM)
    smem = pl.BlockSpec(memory_space=pltpu.SMEM)
    dma = pltpu.SemaphoreType.DMA
    codes, suffix, pre, enc_bias_grad, dec_bias_grad = pl.pallas_call(
        exchange_kernel,
        out_shape=[
            jax.ShapeDtypeStruct((2 * tokens, block), low),
            jax.ShapeDtypeStruct((HALF, 2, SUB, width), low),
            jax.ShapeDtypeStruct((tokens, block), low),
            jax.ShapeDtypeStruct((1, block), full),
            jax.ShapeDtypeStruct((1, width), full),
        ],
        in_specs=[hbm, hbm, hbm, hbm, hbm, hbm, smem],
        out_specs=[hbm, hbm, vmem, vmem, vmem],
        scratch_shapes=[
            pltpu.VMEM((tokens, width), low),
            pltpu.VMEM((width, block), low),
            pltpu.VMEM((1, block), full),
            pltpu.VMEM((block, width), low),
            pltpu.VMEM((1, width), full),
            pltpu.VMEM((tokens, block), jnp.int32),
            pltpu.VMEM((tokens, block), full),
            pltpu.VMEM((tokens, block), full),
            pltpu.VMEM((tokens, block), full),
            pltpu.VMEM((tokens, block), full),
            pltpu.VMEM((2 * tokens, block), low),
            pltpu.VMEM((HALF, 2, SUB, width), low),
            pltpu.VMEM((HALF, 2, SUB, width), low),
            pltpu.VMEM((SUB, width), low),
            pltpu.VMEM((SUB, width), low),
            pltpu.VMEM((5, SUB, width), low),
            pltpu.VMEM((HALF, 2, SUB, width), low),
            pltpu.VMEM((1, width), full),
            pltpu.VMEM((HALF, 1, width), full),
            pltpu.VMEM((1, width), full),
            pltpu.VMEM((1, width), full),
            dma((7,)),
            dma((4,)),
            dma((chunks, HALF)),
            dma((chunks, HALF)),
            dma((chunks + 1,)),
            dma((chunks + 1,)),
            dma((chunks, HALF)),
            dma((chunks, HALF)),
            dma((HALF,)),
            dma((HALF,)),
            dma((1 + chunks,)),
        ],
        compiler_params=pltpu.CompilerParams(
            collective_id=0, has_side_effects=True, vmem_limit_bytes=60 * 1024 * 1024
        ),
        name="exchange",
    )(
        activations, encoder, encoder_bias, decoder, decoder_bias, kept_mask, boundaries,
    )
    suffix = suffix.reshape(2 * tokens, width)
    enc_grad, dec_grad, enc_bias_grad, dec_bias_grad = pl.pallas_call(
        grads_kernel,
        grid=(STEPS,),
        out_shape=[
            jax.ShapeDtypeStruct((width, block), low),
            jax.ShapeDtypeStruct((block, width), low),
            jax.ShapeDtypeStruct((block,), full),
            jax.ShapeDtypeStruct((width,), full),
        ],
        in_specs=[
            pl.BlockSpec((tokens, wide), lambda c: (0, c)),
            pl.BlockSpec((tokens, block), lambda c: (0, 0)),
            pl.BlockSpec((2 * tokens, block), lambda c: (0, 0)),
            pl.BlockSpec((2 * tokens, wide), lambda c: (0, c)),
            pl.BlockSpec((1, block), lambda c: (0, 0)),
            pl.BlockSpec((1, width), lambda c: (0, 0)),
        ],
        out_specs=[
            pl.BlockSpec((wide, block), lambda c: (c, 0)),
            pl.BlockSpec((block, wide), lambda c: (0, c)),
            pl.BlockSpec((block,), lambda c: (0,)),
            pl.BlockSpec((width,), lambda c: (0,)),
        ],
        compiler_params=pltpu.CompilerParams(vmem_limit_bytes=60 * 1024 * 1024),
        name="grads",
    )(activations, pre, codes, suffix, enc_bias_grad, dec_bias_grad)
    return enc_grad, enc_bias_grad, dec_grad, dec_bias_grad


def fits(mesh):
    return mesh.shape["lat"] == 2 * HALF and mesh.shape["wid"] == 2


def solution(mesh):
    placed = (
        P(None, "wid"),
        P("wid", "lat"),
        P("lat"),
        P("lat", "wid"),
        P("wid"),
        P(None, "lat"),
        P(),
    )
    return jax.shard_map(
        kernel_body if fits(mesh) else general_body,
        mesh=mesh,
        in_specs=placed,
        out_specs=(P("wid", "lat"), P("lat"), P("lat", "wid"), P("wid")),
        check_vma=False,
    )
```

```python
import functools

import jax
import jax.numpy as jnp
from jax import lax
from jax.experimental import pallas as pl
from jax.experimental.pallas import tpu as pltpu
from jax.sharding import PartitionSpec as P

GROUPS = 8
HALF = 8
SUB = 16
LANES = 128
AHEAD = 3
PARTS = 2
MESH = pl.DeviceIdType.MESH


def prefix(part, axis, combine, identity, reverse):
    count = lax.axis_size(axis)
    place = lax.axis_index(axis)
    ahead = count - 1 - place if reverse else place
    gathered = lax.all_gather(part, axis)
    state = jnp.zeros_like(part) + jnp.asarray(identity, part.dtype)

    def one(step, state):
        source = count - 1 - step if reverse else step
        return combine(state, lax.dynamic_index_in_dim(gathered, source, 0, False))

    return lax.fori_loop(0, ahead, one, state)


def add_terms(earlier, later):
    return earlier + later


def general_body(activations, encoder, encoder_bias, decoder, decoder_bias, kept_mask, boundaries):
    latent_width = encoder.shape[1]
    first_latent = lax.axis_index("lat") * latent_width
    latent_ids = first_latent + jnp.arange(latent_width, dtype=jnp.int32)
    kept_float = kept_mask.astype(jnp.float32)
    encoder_part = jnp.dot(activations, encoder, preferred_element_type=jnp.float32)
    preacts = lax.psum(encoder_part, "wid") + encoder_bias
    codes = (kept_float * preacts).astype(jnp.bfloat16)
    inside_rows = (boundaries > first_latent) & (boundaries <= first_latent + latent_width)
    holds_cut = jnp.any(inside_rows)
    cut_point = jnp.sum(jnp.where(inside_rows, boundaries, 0))
    below_cut = latent_ids < cut_point
    zero_code = jnp.zeros((), jnp.bfloat16)
    masked_codes = jnp.stack(
        [
            jnp.where(below_cut[None, :], codes, zero_code),
            jnp.where(below_cut[None, :], zero_code, codes),
        ]
    )
    decoded_pieces = jnp.einsum(
        "sbj,jd->sbd", masked_codes, decoder, preferred_element_type=jnp.float32
    )
    local_total = decoded_pieces[0] + decoded_pieces[1]
    zero_rows = jnp.zeros_like(local_total)
    prefix_sum = prefix(local_total, "lat", add_terms, zero_rows, False)
    target_rows = activations.astype(jnp.float32)
    scaled_error = jnp.where(
        holds_cut, (decoder_bias + prefix_sum + decoded_pieces[0] - target_rows) / GROUPS, 0.0
    )
    suffix_sum = prefix(scaled_error, "lat", add_terms, zero_rows, True)
    below_suffix = suffix_sum + scaled_error
    suffix_pair = jnp.stack([below_suffix, suffix_sum]).astype(jnp.bfloat16)
    back_grads = jnp.einsum("sbd,jd->sbj", suffix_pair, decoder, preferred_element_type=jnp.float32)
    partial_grads = jnp.where(below_cut[None, :], back_grads[0], back_grads[1])
    coded_grads = lax.psum(partial_grads, "wid")
    pre_grads = kept_float * coded_grads
    encoder_bias_grad = jnp.sum(pre_grads, axis=0)
    pre_low = pre_grads.astype(jnp.bfloat16)
    encoder_grad = lax.dot_general(
        activations, pre_low, (((0,), (0,)), ((), ())), preferred_element_type=jnp.float32
    ).astype(jnp.bfloat16)
    decoder_grad = jnp.einsum(
        "sbj,sbd->jd", masked_codes, suffix_pair, preferred_element_type=jnp.float32
    ).astype(jnp.bfloat16)
    decoder_bias_grad = lax.psum(jnp.sum(scaled_error, axis=0), "lat")
    return (encoder_grad, encoder_bias_grad, decoder_grad, decoder_bias_grad)


def column_chunks(width):
    tiles = width // LANES
    widths = []
    while tiles > 0:
        widths.append(min(2, tiles))
        tiles -= widths[-1]
    ends = [LANES * sum(widths[: k + 1]) for k in range(len(widths))]
    return [slice(end - LANES * count, end) for end, count in zip(ends, widths)]


def reduce_pieces(pieces, span):
    def piece(source, which):
        return pieces[source, which, :, span].astype(jnp.float32)

    upper = [piece(2 * k, 1) + piece(2 * k + 1, 1) for k in range(4)]
    lower = [piece(2 * k, 0) for k in range(4)]
    segments = [upper[k] + lower[k + 1] for k in range(3)] + [upper[3]]
    return lower[0], segments


def exchange_kernel(
    act_hbm, enc_hbm, enc_bias_hbm, dec_hbm, dec_bias_hbm, mask_hbm, bounds,
    codes_out, suffix_out, pre_out, enc_bias_out, dec_bias_out,
    act, enc, enc_bias, dec, dec_bias, mask, part, part_in, grad, grad_in, codes,
    pieces_out, pieces, cross_out, cross_in, tails, suffix,
    row_out, rows, final_out, final_in, pre_low, enc_bias_row, dec_bias_row,
    load_sems, wid_sems, a_send, a_recv, x_send, x_recv, b_send, b_recv, r_send, r_recv, store_sems,
):
    lat = lax.axis_index("lat")
    wid = lax.axis_index("wid")
    half = lat // HALF
    place = lat % HALF
    even = place % 2 == 0
    odd = place % 2 == 1
    width = act.shape[1]
    spans = column_chunks(width)
    chunks = len(spans)
    views = [pl.ds(span.start, span.stop - span.start) for span in spans]
    block = dec.shape[0]
    other_core = {"lat": lat, "wid": 1 - wid}
    other_half = {"lat": (lat + HALF) % (2 * HALF), "wid": wid}

    def peer(step):
        return (place + step) % HALF

    def source(step):
        return (place + HALF - step) % HALF

    def device(position):
        return {"lat": half * HALF + position, "wid": wid}

    def remote(src, dst, send, recv, target):
        return pltpu.make_async_remote_copy(
            src_ref=src, dst_ref=dst, send_sem=send, recv_sem=recv, device_id=target, device_id_type=MESH
        )

    barrier = pltpu.get_barrier_semaphore()
    for step in range(1, HALF):
        pl.semaphore_signal(barrier, inc=1, device_id=device(peer(step)), device_id_type=MESH)
    pl.semaphore_signal(barrier, inc=1, device_id=other_core, device_id_type=MESH)
    pl.semaphore_signal(barrier, inc=1, device_id=other_half, device_id_type=MESH)

    load_act = pltpu.make_async_copy(act_hbm, act, load_sems.at[0])
    load_act.start()
    load_enc = []
    for c in range(2):
        rows_of = pl.ds(c * (width // 2), width // 2)
        load_enc.append(pltpu.make_async_copy(enc_hbm.at[rows_of], enc.at[rows_of], load_sems.at[1 + c]))
        load_enc[-1].start()
    load_mask = pltpu.make_async_copy(mask_hbm, mask, load_sems.at[3])
    load_mask.start()
    load_enc_bias = pltpu.make_async_copy(enc_bias_hbm, enc_bias.at[0], load_sems.at[4])
    load_enc_bias.start()
    load_dec = pltpu.make_async_copy(dec_hbm, dec, load_sems.at[5])
    load_dec.start()
    load_dec_bias = pltpu.make_async_copy(dec_bias_hbm, dec_bias.at[0], load_sems.at[6])
    load_dec_bias.start()

    @pl.when(odd)
    def _():
        for r in range(HALF):
            suffix[r, 0] = jnp.zeros((SUB, width), jnp.bfloat16)

    load_act.wait()
    total = None
    for c in range(2):
        load_enc[c].wait()
        deep = slice(c * (width // 2), (c + 1) * (width // 2))
        term = jnp.dot(act[:, deep], enc[deep, :], preferred_element_type=jnp.float32)
        total = term if total is None else total + term
    part[...] = total
    pl.semaphore_wait(barrier, HALF + 1)
    swap = remote(part, part_in, wid_sems.at[0], wid_sems.at[1], other_core)
    swap.start()

    first = lat * block
    cut = jnp.int32(0)
    for k in range(GROUPS - 1):
        bound = bounds[k]
        cut = cut + jnp.where((bound > first) & (bound <= first + block), bound, 0)
    tokens = act.shape[0]
    below = (lax.broadcasted_iota(jnp.int32, (tokens, block), 1) + first) < cut
    load_mask.wait()
    load_enc_bias.wait()
    load_dec_bias.wait()
    kept = mask[...].astype(jnp.float32)
    load_dec.wait()
    swap.wait()
    full = kept * ((part[...] + part_in[...]) + enc_bias[...])
    low = jnp.where(below, full, 0.0).astype(jnp.bfloat16)
    high = jnp.where(below, 0.0, full).astype(jnp.bfloat16)
    for r in range(HALF):
        codes[2 * SUB * r : 2 * SUB * r + SUB, :] = low[SUB * r : SUB * (r + 1), :]
        codes[2 * SUB * r + SUB : 2 * SUB * (r + 1), :] = high[SUB * r : SUB * (r + 1), :]
    store_codes = pltpu.make_async_copy(codes, codes_out, store_sems.at[0])
    store_codes.start()

    def send_pieces(c, step, both):
        target = peer(step)
        if both:
            src, dst = pieces_out.at[target, :, :, views[c]], pieces.at[place, :, :, views[c]]
        else:
            src, dst = pieces_out.at[target, 1, :, views[c]], pieces.at[place, 1, :, views[c]]
        return remote(src, dst, a_send.at[c, step], a_recv.at[c, place], device(target))

    def wait_pieces(c, step):
        origin = source(step)

        @pl.when(origin % 2 == 0)
        def _():
            ref = pieces.at[origin, :, :, views[c]]
            remote(ref, ref, a_send.at[c, step], a_recv.at[c, origin], device(origin)).wait_recv()

        @pl.when(origin % 2 == 1)
        def _():
            ref = pieces.at[origin, 1, :, views[c]]
            remote(ref, ref, a_send.at[c, step], a_recv.at[c, origin], device(origin)).wait_recv()

    def make(c):
        span = spans[c]
        made = jnp.dot(codes[...], dec[:, span], preferred_element_type=jnp.float32)
        pieces_out[:, :, :, span] = made.astype(jnp.bfloat16).reshape(HALF, 2, SUB, span.stop - span.start)

        @pl.when(even)
        def _():
            for step in range(1, HALF):
                send_pieces(c, step, True).start()

        @pl.when(odd)
        def _():
            for step in range(1, HALF):
                send_pieces(c, step, False).start()

        pieces[place, :, :, span] = pieces_out[place, :, :, span]

    crossing = []

    def cross(c):
        for step in range(1, HALF):
            wait_pieces(c, step)
        low0, seg = reduce_pieces(pieces, spans[c])
        plain = ((low0 + seg[0]) + seg[1]) + (seg[2] + seg[3])
        weighted = ((5.0 * low0 + 4.0 * seg[0]) + 3.0 * seg[1]) + (2.0 * seg[2] + seg[3])
        cross_out[:, spans[c]] = jnp.where(half == 0, plain, weighted).astype(jnp.bfloat16)
        crossing.append(
            remote(cross_out.at[:, views[c]], cross_in.at[:, views[c]], x_send.at[c], x_recv.at[c], other_half)
        )
        crossing[-1].start()

    def send_suffix(c, step, both):
        target = peer(step)
        if both:
            src, dst = tails.at[pl.ds(target // 2, 2), :, views[c]], suffix.at[place, :, :, views[c]]
        else:
            src, dst = tails.at[target // 2 + 1, :, views[c]], suffix.at[place, 1, :, views[c]]
        return remote(src, dst, b_send.at[c, step], b_recv.at[c, place], device(target))

    later = half.astype(jnp.float32)
    own_rows = pl.ds(pl.multiple_of(place * SUB, SUB), SUB)

    def finalize(c):
        span = spans[c]
        low0, seg = reduce_pieces(pieces, spans[c])
        crossing[c].wait_recv()
        got = cross_in[:, span].astype(jnp.float32)
        base = dec_bias[:, span] - act[own_rows, span].astype(jnp.float32)
        before = base + later * (got + low0)
        errors = []
        running = before
        for k in range(4):
            running = running + seg[k]
            errors.append(running)
        tail = jnp.where(half == 0, 5.0 * errors[3] + got, errors[3])
        scaled = [tail]
        for k in (2, 1, 0):
            tail = tail + errors[k]
            scaled.append(tail)
        scaled.append(tail + before)
        for k in range(5):
            tails[k, :, span] = (scaled[4 - k] / GROUPS).astype(jnp.bfloat16)
        row_out[:, span] = jnp.sum(scaled[3] / GROUPS, axis=0, keepdims=True)
        for step in range(1, HALF):

            @pl.when(peer(step) % 2 == 0)
            def _():
                send_suffix(c, step, True).start()

            @pl.when(peer(step) % 2 == 1)
            def _():
                send_suffix(c, step, False).start()

        suffix[place, :, :, span] = tails[pl.ds(place // 2, 2), :, span]

    for c in range(min(AHEAD, chunks)):
        make(c)
    for c in range(chunks + 1):
        if c < chunks:
            cross(c)
        if c + AHEAD < chunks:
            make(c + AHEAD)
        if c > 0:
            finalize(c - 1)

    def row_copy(step):
        return remote(row_out, rows.at[place], r_send.at[step], r_recv.at[place], device(peer(step)))

    for step in range(1, HALF):
        row_copy(step).start()
    rows[place] = row_out[...]

    back = None
    stores = []
    for c in range(chunks):

        @pl.when(even)
        def _():
            for step in range(1, HALF):
                origin = source(step)
                ref = suffix.at[origin, :, :, views[c]]
                remote(ref, ref, b_send.at[c, step], b_recv.at[c, origin], device(origin)).wait_recv()

        @pl.when(odd)
        def _():
            for step in range(1, HALF):
                origin = source(step)
                ref = suffix.at[origin, 1, :, views[c]]
                remote(ref, ref, b_send.at[c, step], b_recv.at[c, origin], device(origin)).wait_recv()

        span = spans[c]
        there = suffix_out.at[:, :, :, views[c]]
        stores.append(pltpu.make_async_copy(suffix.at[:, :, :, views[c]], there, store_sems.at[1 + c]))
        stores[-1].start()
        term = lax.dot_general(
            suffix[:, :, :, span].reshape(2 * tokens, span.stop - span.start), dec[:, span],
            (((1,), (1,)), ((), ())), preferred_element_type=jnp.float32,
        )
        back = term if back is None else back + term
    pair = back.reshape(HALF, 2, SUB, block)
    below_parts = below.astype(jnp.float32).reshape(HALF, SUB, block) > 0.5
    grad[...] = jnp.where(below_parts, pair[:, 0], pair[:, 1]).reshape(tokens, block)
    swap_back = remote(grad, grad_in, wid_sems.at[2], wid_sems.at[3], other_core)
    swap_back.start()

    for step in range(1, HALF):
        origin = source(step)
        remote(row_out, rows.at[origin], r_send.at[step], r_recv.at[origin], device(origin)).wait_recv()
    summed = rows[0]
    for r in range(1, HALF):
        summed = summed + rows[r]
    final_out[...] = summed
    finish = remote(final_out, final_in, x_send.at[chunks], x_recv.at[chunks], other_half)
    finish.start()

    swap_back.wait()
    pre = kept * (grad[...] + grad_in[...])
    pre_low[...] = pre.astype(jnp.bfloat16)
    stores.append(pltpu.make_async_copy(pre_low, pre_out, store_sems.at[1 + chunks]))
    stores[-1].start()
    enc_bias_row[...] = jnp.sum(pre, axis=0, keepdims=True)
    stores.append(pltpu.make_async_copy(enc_bias_row, enc_bias_out, store_sems.at[2 + chunks]))
    stores[-1].start()

    for c in range(chunks):
        crossing[c].wait_send()

        @pl.when(even)
        def _():
            for step in range(1, HALF):
                send_pieces(c, step, True).wait_send()

        @pl.when(odd)
        def _():
            for step in range(1, HALF):
                send_pieces(c, step, False).wait_send()

        for step in range(1, HALF):

            @pl.when(peer(step) % 2 == 0)
            def _():
                send_suffix(c, step, True).wait_send()

            @pl.when(peer(step) % 2 == 1)
            def _():
                send_suffix(c, step, False).wait_send()

    for step in range(1, HALF):
        row_copy(step).wait_send()
    finish.wait()
    dec_bias_row[...] = jnp.where(half == 0, final_out[...], final_in[...])
    stores.append(pltpu.make_async_copy(dec_bias_row, dec_bias_out, store_sems.at[3 + chunks]))
    stores[-1].start()
    store_codes.wait()
    for store in stores:
        store.wait()


def grads_kernel(
    act_hbm, pre_hbm, codes_hbm, suffix_hbm, enc_bias_in, dec_bias_in,
    enc_out, dec_out, enc_bias_out, dec_bias_out,
    act, pre, codes, suffix, enc_grad, dec_grad, load_sems, store_sems,
):
    contract_rows = (((0,), (0,)), ((), ()))
    width = act.shape[1]
    part = width // PARTS
    pairs = ((pre_hbm, pre), (act_hbm, act), (codes_hbm, codes), (suffix_hbm, suffix))
    loads = [pltpu.make_async_copy(src, dst, load_sems.at[k]) for k, (src, dst) in enumerate(pairs)]
    for load in loads:
        load.start()
    stores = [
        pltpu.make_async_copy(enc_bias_in.at[0], enc_bias_out, store_sems.at[0]),
        pltpu.make_async_copy(dec_bias_in.at[0], dec_bias_out, store_sems.at[1]),
    ]
    for store in stores:
        store.start()

    def put(src, dst):
        stores.append(pltpu.make_async_copy(src, dst, store_sems.at[len(stores)]))
        stores[-1].start()

    loads[0].wait()
    loads[1].wait()
    for k in range(PARTS):
        span, view = slice(k * part, (k + 1) * part), pl.ds(k * part, part)
        enc_grad[span, :] = lax.dot_general(
            act[:, span], pre[...], contract_rows, preferred_element_type=jnp.float32
        ).astype(jnp.bfloat16)
        put(enc_grad.at[view, :], enc_out.at[view, :])
    loads[2].wait()
    loads[3].wait()
    for k in range(PARTS):
        span, view = slice(k * part, (k + 1) * part), pl.ds(k * part, part)
        dec_grad[:, span] = lax.dot_general(
            codes[...], suffix[:, span], contract_rows, preferred_element_type=jnp.float32
        ).astype(jnp.bfloat16)
        put(dec_grad.at[:, view], dec_out.at[:, view])
    for store in stores:
        store.wait()


def kernel_body(activations, encoder, encoder_bias, decoder, decoder_bias, kept_mask, boundaries):
    tokens, width = activations.shape
    block = encoder.shape[1]
    chunks = len(column_chunks(width))
    low, full = jnp.bfloat16, jnp.float32
    hbm = pl.BlockSpec(memory_space=pltpu.HBM)
    smem = pl.BlockSpec(memory_space=pltpu.SMEM)
    dma = pltpu.SemaphoreType.DMA
    codes, suffix, pre, enc_bias_grad, dec_bias_grad = pl.pallas_call(
        exchange_kernel,
        out_shape=[
            jax.ShapeDtypeStruct((2 * tokens, block), low),
            jax.ShapeDtypeStruct((HALF, 2, SUB, width), low),
            jax.ShapeDtypeStruct((tokens, block), low),
            jax.ShapeDtypeStruct((1, block), full),
            jax.ShapeDtypeStruct((1, width), full),
        ],
        in_specs=[hbm, hbm, hbm, hbm, hbm, hbm, smem],
        out_specs=[hbm, hbm, hbm, hbm, hbm],
        scratch_shapes=[
            pltpu.VMEM((tokens, width), low),
            pltpu.VMEM((width, block), low),
            pltpu.VMEM((1, block), full),
            pltpu.VMEM((block, width), low),
            pltpu.VMEM((1, width), full),
            pltpu.VMEM((tokens, block), jnp.int32),
            pltpu.VMEM((tokens, block), full),
            pltpu.VMEM((tokens, block), full),
            pltpu.VMEM((tokens, block), full),
            pltpu.VMEM((tokens, block), full),
            pltpu.VMEM((2 * tokens, block), low),
            pltpu.VMEM((HALF, 2, SUB, width), low),
            pltpu.VMEM((HALF, 2, SUB, width), low),
            pltpu.VMEM((SUB, width), low),
            pltpu.VMEM((SUB, width), low),
            pltpu.VMEM((5, SUB, width), low),
            pltpu.VMEM((HALF, 2, SUB, width), low),
            pltpu.VMEM((1, width), full),
            pltpu.VMEM((HALF, 1, width), full),
            pltpu.VMEM((1, width), full),
            pltpu.VMEM((1, width), full),
            pltpu.VMEM((tokens, block), low),
            pltpu.VMEM((1, block), full),
            pltpu.VMEM((1, width), full),
            dma((7,)),
            dma((4,)),
            dma((chunks, HALF)),
            dma((chunks, HALF)),
            dma((chunks + 1,)),
            dma((chunks + 1,)),
            dma((chunks, HALF)),
            dma((chunks, HALF)),
            dma((HALF,)),
            dma((HALF,)),
            dma((4 + chunks,)),
        ],
        compiler_params=pltpu.CompilerParams(
            collective_id=0, has_side_effects=True, vmem_limit_bytes=60 * 1024 * 1024
        ),
        name="exchange",
    )(
        activations, encoder, encoder_bias, decoder, decoder_bias, kept_mask, boundaries,
    )
    suffix = suffix.reshape(2 * tokens, width)
    enc_grad, dec_grad, enc_bias_grad, dec_bias_grad = pl.pallas_call(
        grads_kernel,
        out_shape=[
            jax.ShapeDtypeStruct((width, block), low),
            jax.ShapeDtypeStruct((block, width), low),
            jax.ShapeDtypeStruct((block,), full),
            jax.ShapeDtypeStruct((width,), full),
        ],
        in_specs=[hbm] * 6,
        out_specs=[hbm] * 4,
        scratch_shapes=[
            pltpu.VMEM((tokens, width), low),
            pltpu.VMEM((tokens, block), low),
            pltpu.VMEM((2 * tokens, block), low),
            pltpu.VMEM((2 * tokens, width), low),
            pltpu.VMEM((width, block), low),
            pltpu.VMEM((block, width), low),
            dma((4,)),
            dma((2 + 2 * PARTS,)),
        ],
        compiler_params=pltpu.CompilerParams(vmem_limit_bytes=60 * 1024 * 1024),
        name="grads",
    )(activations, pre, codes, suffix, enc_bias_grad, dec_bias_grad)
    return enc_grad, enc_bias_grad, dec_grad, dec_bias_grad


def fits(mesh):
    return mesh.shape["lat"] == 2 * HALF and mesh.shape["wid"] == 2


def solution(mesh):
    placed = (
        P(None, "wid"),
        P("wid", "lat"),
        P("lat"),
        P("lat", "wid"),
        P("wid"),
        P(None, "lat"),
        P(),
    )
    return jax.shard_map(
        kernel_body if fits(mesh) else general_body,
        mesh=mesh,
        in_specs=placed,
        out_specs=(P("wid", "lat"), P("lat"), P("lat", "wid"), P("wid")),
        check_vma=False,
    )
```

```python
import functools

import jax
import jax.numpy as jnp
from jax import lax
from jax.experimental import pallas as pl
from jax.experimental.pallas import tpu as pltpu
from jax.sharding import PartitionSpec as P

GROUPS = 8
HALF = 8
SUB = 16
LANES = 128
PARTS = 2
MESH = pl.DeviceIdType.MESH


def prefix(part, axis, combine, identity, reverse):
    count = lax.axis_size(axis)
    place = lax.axis_index(axis)
    ahead = count - 1 - place if reverse else place
    gathered = lax.all_gather(part, axis)
    state = jnp.zeros_like(part) + jnp.asarray(identity, part.dtype)

    def one(step, state):
        source = count - 1 - step if reverse else step
        return combine(state, lax.dynamic_index_in_dim(gathered, source, 0, False))

    return lax.fori_loop(0, ahead, one, state)


def add_terms(earlier, later):
    return earlier + later


def general_body(activations, encoder, encoder_bias, decoder, decoder_bias, kept_mask, boundaries):
    latent_width = encoder.shape[1]
    first_latent = lax.axis_index("lat") * latent_width
    latent_ids = first_latent + jnp.arange(latent_width, dtype=jnp.int32)
    kept_float = kept_mask.astype(jnp.float32)
    encoder_part = jnp.dot(activations, encoder, preferred_element_type=jnp.float32)
    preacts = lax.psum(encoder_part, "wid") + encoder_bias
    codes = (kept_float * preacts).astype(jnp.bfloat16)
    inside_rows = (boundaries > first_latent) & (boundaries <= first_latent + latent_width)
    holds_cut = jnp.any(inside_rows)
    cut_point = jnp.sum(jnp.where(inside_rows, boundaries, 0))
    below_cut = latent_ids < cut_point
    zero_code = jnp.zeros((), jnp.bfloat16)
    masked_codes = jnp.stack(
        [
            jnp.where(below_cut[None, :], codes, zero_code),
            jnp.where(below_cut[None, :], zero_code, codes),
        ]
    )
    decoded_pieces = jnp.einsum(
        "sbj,jd->sbd", masked_codes, decoder, preferred_element_type=jnp.float32
    )
    local_total = decoded_pieces[0] + decoded_pieces[1]
    zero_rows = jnp.zeros_like(local_total)
    prefix_sum = prefix(local_total, "lat", add_terms, zero_rows, False)
    target_rows = activations.astype(jnp.float32)
    scaled_error = jnp.where(
        holds_cut, (decoder_bias + prefix_sum + decoded_pieces[0] - target_rows) / GROUPS, 0.0
    )
    suffix_sum = prefix(scaled_error, "lat", add_terms, zero_rows, True)
    below_suffix = suffix_sum + scaled_error
    suffix_pair = jnp.stack([below_suffix, suffix_sum]).astype(jnp.bfloat16)
    back_grads = jnp.einsum("sbd,jd->sbj", suffix_pair, decoder, preferred_element_type=jnp.float32)
    partial_grads = jnp.where(below_cut[None, :], back_grads[0], back_grads[1])
    coded_grads = lax.psum(partial_grads, "wid")
    pre_grads = kept_float * coded_grads
    encoder_bias_grad = jnp.sum(pre_grads, axis=0)
    pre_low = pre_grads.astype(jnp.bfloat16)
    encoder_grad = lax.dot_general(
        activations, pre_low, (((0,), (0,)), ((), ())), preferred_element_type=jnp.float32
    ).astype(jnp.bfloat16)
    decoder_grad = jnp.einsum(
        "sbj,sbd->jd", masked_codes, suffix_pair, preferred_element_type=jnp.float32
    ).astype(jnp.bfloat16)
    decoder_bias_grad = lax.psum(jnp.sum(scaled_error, axis=0), "lat")
    return (encoder_grad, encoder_bias_grad, decoder_grad, decoder_bias_grad)


def column_chunks(width):
    tiles = width // LANES
    widths = []
    while tiles > 0:
        widths.append(min(4 if len(widths) in (1, 2) else 2, tiles))
        tiles -= widths[-1]
    ends = [LANES * sum(widths[: k + 1]) for k in range(len(widths))]
    return [slice(end - LANES * count, end) for end, count in zip(ends, widths)]


def reduce_pieces(pieces, span):
    def piece(source, which):
        return pieces[source, which, :, span].astype(jnp.float32)

    upper = [piece(2 * k, 1) + piece(2 * k + 1, 1) for k in range(4)]
    lower = [piece(2 * k, 0) for k in range(4)]
    segments = [upper[k] + lower[k + 1] for k in range(3)] + [upper[3]]
    return lower[0], segments


def exchange_kernel(
    act_hbm, enc_hbm, enc_bias_hbm, dec_hbm, dec_bias_hbm, mask_hbm, bounds,
    act_out, dec_grad_out, pre_out, enc_bias_out, dec_bias_out,
    act, enc, enc_bias, dec, dec_bias, mask, part, part_in, grad, grad_in, codes,
    pieces_out, pieces, cross_out, cross_in, tails, suffix,
    row_out, rows, final_out, final_in, pre_low, enc_bias_row, dec_bias_row,
    act_turned, codes_turned, dec_grad,
    load_sems, wid_sems, a_send, a_recv, x_send, x_recv, b_send, b_recv, r_send, r_recv, store_sems,
):
    lat = lax.axis_index("lat")
    wid = lax.axis_index("wid")
    half = lat // HALF
    place = lat % HALF
    even = place % 2 == 0
    odd = place % 2 == 1
    width = act.shape[1]
    spans = column_chunks(width)
    chunks = len(spans)
    views = [pl.ds(span.start, span.stop - span.start) for span in spans]
    block = dec.shape[0]
    halves = [slice(0, block // 2), slice(block // 2, block)]
    sides = [pl.ds(0, block // 2), pl.ds(block // 2, block // 2)]
    other_core = {"lat": lat, "wid": 1 - wid}
    other_half = {"lat": (lat + HALF) % (2 * HALF), "wid": wid}

    def peer(step):
        return (place + step) % HALF

    def source(step):
        return (place + HALF - step) % HALF

    def device(position):
        return {"lat": half * HALF + position, "wid": wid}

    def remote(src, dst, send, recv, target):
        return pltpu.make_async_remote_copy(
            src_ref=src, dst_ref=dst, send_sem=send, recv_sem=recv, device_id=target, device_id_type=MESH
        )

    barrier = pltpu.get_barrier_semaphore()
    for step in range(1, HALF):
        pl.semaphore_signal(barrier, inc=1, device_id=device(peer(step)), device_id_type=MESH)
    pl.semaphore_signal(barrier, inc=1, device_id=other_core, device_id_type=MESH)
    pl.semaphore_signal(barrier, inc=1, device_id=other_half, device_id_type=MESH)

    load_act = pltpu.make_async_copy(act_hbm, act, load_sems.at[0])
    load_act.start()
    load_enc = []
    for c in range(2):
        load_enc.append(pltpu.make_async_copy(enc_hbm.at[:, sides[c]], enc.at[:, sides[c]], load_sems.at[1 + c]))
        load_enc[-1].start()
    load_mask = pltpu.make_async_copy(mask_hbm, mask, load_sems.at[3])
    load_mask.start()
    load_enc_bias = pltpu.make_async_copy(enc_bias_hbm, enc_bias.at[0], load_sems.at[4])
    load_enc_bias.start()
    load_dec = pltpu.make_async_copy(dec_hbm, dec, load_sems.at[5])
    load_dec.start()
    load_dec_bias = pltpu.make_async_copy(dec_bias_hbm, dec_bias.at[0], load_sems.at[6])
    load_dec_bias.start()

    @pl.when(odd)
    def _():
        for r in range(HALF):
            suffix[r, 0] = jnp.zeros((SUB, width), jnp.bfloat16)

    load_act.wait()
    swaps = []
    for c in range(2):
        load_enc[c].wait()
        part[:, halves[c]] = jnp.dot(act[...], enc[:, halves[c]], preferred_element_type=jnp.float32)
        if c == 0:
            pl.semaphore_wait(barrier, HALF + 1)
        here, there = part.at[:, sides[c]], part_in.at[:, sides[c]]
        swaps.append(remote(here, there, wid_sems.at[2 * c], wid_sems.at[2 * c + 1], other_core))
        swaps[-1].start()

    first = lat * block
    cut = jnp.int32(0)
    for k in range(GROUPS - 1):
        bound = bounds[k]
        cut = cut + jnp.where((bound > first) & (bound <= first + block), bound, 0)
    tokens = act.shape[0]
    below = (lax.broadcasted_iota(jnp.int32, (tokens, block), 1) + first) < cut
    load_mask.wait()
    load_enc_bias.wait()
    load_dec_bias.wait()
    kept = mask[...].astype(jnp.float32)
    load_dec.wait()
    for swap in swaps:
        swap.wait()
    full = kept * ((part[...] + part_in[...]) + enc_bias[...])
    low = jnp.where(below, full, 0.0).astype(jnp.bfloat16)
    high = jnp.where(below, 0.0, full).astype(jnp.bfloat16)
    for r in range(HALF):
        codes[2 * SUB * r : 2 * SUB * r + SUB, :] = low[SUB * r : SUB * (r + 1), :]
        codes[2 * SUB * r + SUB : 2 * SUB * (r + 1), :] = high[SUB * r : SUB * (r + 1), :]

    def send_pieces(c, step, both):
        target = peer(step)
        if both:
            src, dst = pieces_out.at[target, :, :, views[c]], pieces.at[place, :, :, views[c]]
        else:
            src, dst = pieces_out.at[target, 1, :, views[c]], pieces.at[place, 1, :, views[c]]
        return remote(src, dst, a_send.at[c, step], a_recv.at[c, place], device(target))

    def wait_pieces(c, step):
        origin = source(step)

        @pl.when(origin % 2 == 0)
        def _():
            ref = pieces.at[origin, :, :, views[c]]
            remote(ref, ref, a_send.at[c, step], a_recv.at[c, origin], device(origin)).wait_recv()

        @pl.when(origin % 2 == 1)
        def _():
            ref = pieces.at[origin, 1, :, views[c]]
            remote(ref, ref, a_send.at[c, step], a_recv.at[c, origin], device(origin)).wait_recv()

    def make(c):
        span = spans[c]
        made = jnp.dot(codes[...], dec[:, span], preferred_element_type=jnp.float32)
        pieces_out[:, :, :, span] = made.astype(jnp.bfloat16).reshape(HALF, 2, SUB, span.stop - span.start)

        @pl.when(even)
        def _():
            for step in range(1, HALF):
                send_pieces(c, step, True).start()

        @pl.when(odd)
        def _():
            for step in range(1, HALF):
                send_pieces(c, step, False).start()

        pieces[place, :, :, span] = pieces_out[place, :, :, span]

    crossing = []

    def cross(c):
        for step in range(1, HALF):
            wait_pieces(c, step)
        low0, seg = reduce_pieces(pieces, spans[c])
        plain = ((low0 + seg[0]) + seg[1]) + (seg[2] + seg[3])
        weighted = ((5.0 * low0 + 4.0 * seg[0]) + 3.0 * seg[1]) + (2.0 * seg[2] + seg[3])
        cross_out[:, spans[c]] = jnp.where(half == 0, plain, weighted).astype(jnp.bfloat16)
        crossing.append(
            remote(cross_out.at[:, views[c]], cross_in.at[:, views[c]], x_send.at[c], x_recv.at[c], other_half)
        )
        crossing[-1].start()

    def send_suffix(c, step, both):
        target = peer(step)
        if both:
            src, dst = tails.at[pl.ds(target // 2, 2), :, views[c]], suffix.at[place, :, :, views[c]]
        else:
            src, dst = tails.at[target // 2 + 1, :, views[c]], suffix.at[place, 1, :, views[c]]
        return remote(src, dst, b_send.at[c, step], b_recv.at[c, place], device(target))

    later = half.astype(jnp.float32)
    own_rows = pl.ds(pl.multiple_of(place * SUB, SUB), SUB)

    def finalize(c):
        span = spans[c]
        low0, seg = reduce_pieces(pieces, spans[c])
        crossing[c].wait_recv()
        got = cross_in[:, span].astype(jnp.float32)
        base = dec_bias[:, span] - act[own_rows, span].astype(jnp.float32)
        before = base + later * (got + low0)
        errors = []
        running = before
        for k in range(4):
            running = running + seg[k]
            errors.append(running)
        tail = jnp.where(half == 0, 5.0 * errors[3] + got, errors[3])
        scaled = [tail]
        for k in (2, 1, 0):
            tail = tail + errors[k]
            scaled.append(tail)
        scaled.append(tail + before)
        for k in range(5):
            tails[k, :, span] = (scaled[4 - k] / GROUPS).astype(jnp.bfloat16)
        row_out[:, span] = jnp.sum(scaled[3] / GROUPS, axis=0, keepdims=True)
        for step in range(1, HALF):

            @pl.when(peer(step) % 2 == 0)
            def _():
                send_suffix(c, step, True).start()

            @pl.when(peer(step) % 2 == 1)
            def _():
                send_suffix(c, step, False).start()

        suffix[place, :, :, span] = tails[pl.ds(place // 2, 2), :, span]

    for c in range(chunks):
        make(c)
    act_turned[...] = act[...].T
    stores = [pltpu.make_async_copy(act_turned, act_out, store_sems.at[1])]
    stores[0].start()
    codes_turned[...] = codes[...].T
    for c in range(chunks + 1):
        if c < chunks:
            cross(c)
        if c > 0:
            finalize(c - 1)

    def row_copy(step):
        return remote(row_out, rows.at[place], r_send.at[step], r_recv.at[place], device(peer(step)))

    for step in range(1, HALF):
        row_copy(step).start()
    rows[place] = row_out[...]

    below_parts = below.astype(jnp.float32).reshape(HALF, SUB, block) > 0.5
    back = [None, None]
    swaps_back = []

    def grad_columns(c):
        span = spans[c]
        both = suffix[:, :, :, span].reshape(2 * tokens, span.stop - span.start)
        dec_grad[:, span] = jnp.dot(codes_turned[...], both, preferred_element_type=jnp.float32).astype(jnp.bfloat16)
        stores.append(pltpu.make_async_copy(dec_grad.at[:, views[c]], dec_grad_out.at[:, views[c]], store_sems.at[5 + c]))
        stores[-1].start()

    for c in range(chunks):

        @pl.when(even)
        def _():
            for step in range(1, HALF):
                origin = source(step)
                ref = suffix.at[origin, :, :, views[c]]
                remote(ref, ref, b_send.at[c, step], b_recv.at[c, origin], device(origin)).wait_recv()

        @pl.when(odd)
        def _():
            for step in range(1, HALF):
                origin = source(step)
                ref = suffix.at[origin, 1, :, views[c]]
                remote(ref, ref, b_send.at[c, step], b_recv.at[c, origin], device(origin)).wait_recv()

        span = spans[c]
        both = suffix[:, :, :, span].reshape(2 * tokens, span.stop - span.start)
        for side in range(2):
            term = lax.dot_general(
                both, dec[halves[side], span], (((1,), (1,)), ((), ())), preferred_element_type=jnp.float32
            )
            back[side] = term if back[side] is None else back[side] + term
            if c == chunks - 1:
                pair = back[side].reshape(HALF, 2, SUB, block // 2)
                chosen = jnp.where(below_parts[:, :, halves[side]], pair[:, 0], pair[:, 1])
                grad[:, halves[side]] = chosen.reshape(tokens, block // 2)
                here, there = grad.at[:, sides[side]], grad_in.at[:, sides[side]]
                swaps_back.append(
                    remote(here, there, wid_sems.at[4 + 2 * side], wid_sems.at[5 + 2 * side], other_core)
                )
                swaps_back[-1].start()
        if c < chunks - 2:
            grad_columns(c)

    for c in range(chunks - 2, chunks):
        grad_columns(c)

    for step in range(1, HALF):
        origin = source(step)
        remote(row_out, rows.at[origin], r_send.at[step], r_recv.at[origin], device(origin)).wait_recv()
    summed = rows[0]
    for r in range(1, HALF):
        summed = summed + rows[r]
    final_out[...] = summed
    finish = remote(final_out, final_in, x_send.at[chunks], x_recv.at[chunks], other_half)
    finish.start()

    for swap in swaps_back:
        swap.wait()
    pre = kept * (grad[...] + grad_in[...])
    pre_low[...] = pre.astype(jnp.bfloat16)
    stores.append(pltpu.make_async_copy(pre_low, pre_out, store_sems.at[2]))
    stores[-1].start()
    enc_bias_row[...] = jnp.sum(pre, axis=0, keepdims=True)
    stores.append(pltpu.make_async_copy(enc_bias_row, enc_bias_out, store_sems.at[3]))
    stores[-1].start()

    for c in range(chunks):
        crossing[c].wait_send()

        @pl.when(even)
        def _():
            for step in range(1, HALF):
                send_pieces(c, step, True).wait_send()

        @pl.when(odd)
        def _():
            for step in range(1, HALF):
                send_pieces(c, step, False).wait_send()

        for step in range(1, HALF):

            @pl.when(peer(step) % 2 == 0)
            def _():
                send_suffix(c, step, True).wait_send()

            @pl.when(peer(step) % 2 == 1)
            def _():
                send_suffix(c, step, False).wait_send()

    for step in range(1, HALF):
        row_copy(step).wait_send()
    finish.wait()
    dec_bias_row[...] = jnp.where(half == 0, final_out[...], final_in[...])
    stores.append(pltpu.make_async_copy(dec_bias_row, dec_bias_out, store_sems.at[4]))
    stores[-1].start()
    for store in stores:
        store.wait()


def grads_kernel(
    act_hbm, pre_hbm, dec_grad_in, enc_bias_in, dec_bias_in,
    enc_out, dec_out, enc_bias_out, dec_bias_out,
    act, pre, enc_grad, load_sems, store_sems,
):
    part = act.shape[0] // PARTS
    loads = [
        pltpu.make_async_copy(pre_hbm, pre, load_sems.at[0]),
        pltpu.make_async_copy(act_hbm, act, load_sems.at[1]),
    ]
    stores = [
        pltpu.make_async_copy(dec_grad_in, dec_out, store_sems.at[0]),
        pltpu.make_async_copy(enc_bias_in.at[0], enc_bias_out, store_sems.at[1]),
        pltpu.make_async_copy(dec_bias_in.at[0], dec_bias_out, store_sems.at[2]),
    ]
    for copy in loads + stores:
        copy.start()
    for load in loads:
        load.wait()
    for k in range(PARTS):
        span, view = slice(k * part, (k + 1) * part), pl.ds(k * part, part)
        enc_grad[span, :] = jnp.dot(act[span, :], pre[...], preferred_element_type=jnp.float32).astype(jnp.bfloat16)
        stores.append(pltpu.make_async_copy(enc_grad.at[view, :], enc_out.at[view, :], store_sems.at[3 + k]))
        stores[-1].start()
    for store in stores:
        store.wait()


def kernel_body(activations, encoder, encoder_bias, decoder, decoder_bias, kept_mask, boundaries):
    tokens, width = activations.shape
    block = encoder.shape[1]
    chunks = len(column_chunks(width))
    low, full = jnp.bfloat16, jnp.float32
    hbm = pl.BlockSpec(memory_space=pltpu.HBM)
    smem = pl.BlockSpec(memory_space=pltpu.SMEM)
    dma = pltpu.SemaphoreType.DMA
    act_turned, dec_grad, pre, enc_bias_grad, dec_bias_grad = pl.pallas_call(
        exchange_kernel,
        out_shape=[
            jax.ShapeDtypeStruct((width, tokens), low),
            jax.ShapeDtypeStruct((block, width), low),
            jax.ShapeDtypeStruct((tokens, block), low),
            jax.ShapeDtypeStruct((1, block), full),
            jax.ShapeDtypeStruct((1, width), full),
        ],
        in_specs=[hbm, hbm, hbm, hbm, hbm, hbm, smem],
        out_specs=[hbm, hbm, hbm, hbm, hbm],
        scratch_shapes=[
            pltpu.VMEM((tokens, width), low),
            pltpu.VMEM((width, block), low),
            pltpu.VMEM((1, block), full),
            pltpu.VMEM((block, width), low),
            pltpu.VMEM((1, width), full),
            pltpu.VMEM((tokens, block), jnp.int32),
            pltpu.VMEM((tokens, block), full),
            pltpu.VMEM((tokens, block), full),
            pltpu.VMEM((tokens, block), full),
            pltpu.VMEM((tokens, block), full),
            pltpu.VMEM((2 * tokens, block), low),
            pltpu.VMEM((HALF, 2, SUB, width), low),
            pltpu.VMEM((HALF, 2, SUB, width), low),
            pltpu.VMEM((SUB, width), low),
            pltpu.VMEM((SUB, width), low),
            pltpu.VMEM((5, SUB, width), low),
            pltpu.VMEM((HALF, 2, SUB, width), low),
            pltpu.VMEM((1, width), full),
            pltpu.VMEM((HALF, 1, width), full),
            pltpu.VMEM((1, width), full),
            pltpu.VMEM((1, width), full),
            pltpu.VMEM((tokens, block), low),
            pltpu.VMEM((1, block), full),
            pltpu.VMEM((1, width), full),
            pltpu.VMEM((width, tokens), low),
            pltpu.VMEM((block, 2 * tokens), low),
            pltpu.VMEM((block, width), low),
            dma((7,)),
            dma((8,)),
            dma((chunks, HALF)),
            dma((chunks, HALF)),
            dma((chunks + 1,)),
            dma((chunks + 1,)),
            dma((chunks, HALF)),
            dma((chunks, HALF)),
            dma((HALF,)),
            dma((HALF,)),
            dma((5 + chunks,)),
        ],
        compiler_params=pltpu.CompilerParams(
            collective_id=0, has_side_effects=True, vmem_limit_bytes=60 * 1024 * 1024
        ),
        name="exchange",
    )(
        activations, encoder, encoder_bias, decoder, decoder_bias, kept_mask, boundaries,
    )
    enc_grad, dec_grad, enc_bias_grad, dec_bias_grad = pl.pallas_call(
        grads_kernel,
        out_shape=[
            jax.ShapeDtypeStruct((width, block), low),
            jax.ShapeDtypeStruct((block, width), low),
            jax.ShapeDtypeStruct((block,), full),
            jax.ShapeDtypeStruct((width,), full),
        ],
        in_specs=[hbm] * 5,
        out_specs=[hbm] * 4,
        scratch_shapes=[
            pltpu.VMEM((width, tokens), low),
            pltpu.VMEM((tokens, block), low),
            pltpu.VMEM((width, block), low),
            dma((2,)),
            dma((3 + PARTS,)),
        ],
        compiler_params=pltpu.CompilerParams(vmem_limit_bytes=60 * 1024 * 1024),
        name="grads",
    )(act_turned, pre, dec_grad, enc_bias_grad, dec_bias_grad)
    return enc_grad, enc_bias_grad, dec_grad, dec_bias_grad


def fits(mesh):
    return mesh.shape["lat"] == 2 * HALF and mesh.shape["wid"] == 2


def solution(mesh):
    placed = (
        P(None, "wid"),
        P("wid", "lat"),
        P("lat"),
        P("lat", "wid"),
        P("wid"),
        P(None, "lat"),
        P(),
    )
    return jax.shard_map(
        kernel_body if fits(mesh) else general_body,
        mesh=mesh,
        in_specs=placed,
        out_specs=(P("wid", "lat"), P("lat"), P("lat", "wid"), P("wid")),
        check_vma=False,
    )
```

```python
import functools

import jax
import jax.numpy as jnp
from jax import lax
from jax.experimental import pallas as pl
from jax.experimental.pallas import tpu as pltpu
from jax.sharding import PartitionSpec as P

GROUPS = 8
HALF = 8
SUB = 16
LANES = 128
PARTS = 2
MESH = pl.DeviceIdType.MESH


def prefix(part, axis, combine, identity, reverse):
    count = lax.axis_size(axis)
    place = lax.axis_index(axis)
    ahead = count - 1 - place if reverse else place
    gathered = lax.all_gather(part, axis)
    state = jnp.zeros_like(part) + jnp.asarray(identity, part.dtype)

    def one(step, state):
        source = count - 1 - step if reverse else step
        return combine(state, lax.dynamic_index_in_dim(gathered, source, 0, False))

    return lax.fori_loop(0, ahead, one, state)


def add_terms(earlier, later):
    return earlier + later


def general_body(activations, encoder, encoder_bias, decoder, decoder_bias, kept_mask, boundaries):
    latent_width = encoder.shape[1]
    first_latent = lax.axis_index("lat") * latent_width
    latent_ids = first_latent + jnp.arange(latent_width, dtype=jnp.int32)
    kept_float = kept_mask.astype(jnp.float32)
    encoder_part = jnp.dot(activations, encoder, preferred_element_type=jnp.float32)
    preacts = lax.psum(encoder_part, "wid") + encoder_bias
    codes = (kept_float * preacts).astype(jnp.bfloat16)
    inside_rows = (boundaries > first_latent) & (boundaries <= first_latent + latent_width)
    holds_cut = jnp.any(inside_rows)
    cut_point = jnp.sum(jnp.where(inside_rows, boundaries, 0))
    below_cut = latent_ids < cut_point
    zero_code = jnp.zeros((), jnp.bfloat16)
    masked_codes = jnp.stack(
        [
            jnp.where(below_cut[None, :], codes, zero_code),
            jnp.where(below_cut[None, :], zero_code, codes),
        ]
    )
    decoded_pieces = jnp.einsum(
        "sbj,jd->sbd", masked_codes, decoder, preferred_element_type=jnp.float32
    )
    local_total = decoded_pieces[0] + decoded_pieces[1]
    zero_rows = jnp.zeros_like(local_total)
    prefix_sum = prefix(local_total, "lat", add_terms, zero_rows, False)
    target_rows = activations.astype(jnp.float32)
    scaled_error = jnp.where(
        holds_cut, (decoder_bias + prefix_sum + decoded_pieces[0] - target_rows) / GROUPS, 0.0
    )
    suffix_sum = prefix(scaled_error, "lat", add_terms, zero_rows, True)
    below_suffix = suffix_sum + scaled_error
    suffix_pair = jnp.stack([below_suffix, suffix_sum]).astype(jnp.bfloat16)
    back_grads = jnp.einsum("sbd,jd->sbj", suffix_pair, decoder, preferred_element_type=jnp.float32)
    partial_grads = jnp.where(below_cut[None, :], back_grads[0], back_grads[1])
    coded_grads = lax.psum(partial_grads, "wid")
    pre_grads = kept_float * coded_grads
    encoder_bias_grad = jnp.sum(pre_grads, axis=0)
    pre_low = pre_grads.astype(jnp.bfloat16)
    encoder_grad = lax.dot_general(
        activations, pre_low, (((0,), (0,)), ((), ())), preferred_element_type=jnp.float32
    ).astype(jnp.bfloat16)
    decoder_grad = jnp.einsum(
        "sbj,sbd->jd", masked_codes, suffix_pair, preferred_element_type=jnp.float32
    ).astype(jnp.bfloat16)
    decoder_bias_grad = lax.psum(jnp.sum(scaled_error, axis=0), "lat")
    return (encoder_grad, encoder_bias_grad, decoder_grad, decoder_bias_grad)


def column_chunks(width):
    tiles = width // LANES
    widths = []
    while tiles > 0:
        widths.append(min(4 if len(widths) in (1, 2) else 2, tiles))
        tiles -= widths[-1]
    ends = [LANES * sum(widths[: k + 1]) for k in range(len(widths))]
    return [slice(end - LANES * count, end) for end, count in zip(ends, widths)]


def reduce_pieces(pieces, span):
    def piece(source, which):
        return pieces[source, which, :, span].astype(jnp.float32)

    upper = [piece(2 * k, 1) + piece(2 * k + 1, 1) for k in range(4)]
    lower = [piece(2 * k, 0) for k in range(4)]
    segments = [upper[k] + lower[k + 1] for k in range(3)] + [upper[3]]
    return lower[0], segments


def exchange_kernel(
    act_hbm, enc_hbm, enc_bias_hbm, dec_hbm, dec_bias_hbm, mask_hbm, bounds,
    act_out, dec_grad_out, pre_out, enc_bias_out, dec_bias_out,
    act, enc, enc_bias, dec, dec_bias, mask, part, part_in, grad, grad_in, codes,
    pieces_out, pieces, cross_out, cross_in, tails, suffix,
    row_out, rows, final_out, final_in, pre_low, enc_bias_row, dec_bias_row,
    act_turned, codes_turned, dec_grad,
    load_sems, wid_sems, a_send, a_recv, x_send, x_recv, b_send, b_recv, r_send, r_recv, store_sems,
):
    lat = lax.axis_index("lat")
    wid = lax.axis_index("wid")
    half = lat // HALF
    place = lat % HALF
    even = place % 2 == 0
    odd = place % 2 == 1
    width = act.shape[1]
    spans = column_chunks(width)
    chunks = len(spans)
    views = [pl.ds(span.start, span.stop - span.start) for span in spans]
    block = dec.shape[0]
    halves = [slice(0, block // 2), slice(block // 2, block)]
    sides = [pl.ds(0, block // 2), pl.ds(block // 2, block // 2)]
    other_core = {"lat": lat, "wid": 1 - wid}
    other_half = {"lat": (lat + HALF) % (2 * HALF), "wid": wid}

    def peer(step):
        return (place + step) % HALF

    def source(step):
        return (place + HALF - step) % HALF

    def device(position):
        return {"lat": half * HALF + position, "wid": wid}

    def remote(src, dst, send, recv, target):
        return pltpu.make_async_remote_copy(
            src_ref=src, dst_ref=dst, send_sem=send, recv_sem=recv, device_id=target, device_id_type=MESH
        )

    barrier = pltpu.get_barrier_semaphore()
    for step in range(1, HALF):
        pl.semaphore_signal(barrier, inc=1, device_id=device(peer(step)), device_id_type=MESH)
    pl.semaphore_signal(barrier, inc=1, device_id=other_core, device_id_type=MESH)
    pl.semaphore_signal(barrier, inc=1, device_id=other_half, device_id_type=MESH)

    load_act = pltpu.make_async_copy(act_hbm, act, load_sems.at[0])
    load_act.start()
    load_enc = []
    for c in range(2):
        load_enc.append(pltpu.make_async_copy(enc_hbm.at[:, sides[c]], enc.at[:, sides[c]], load_sems.at[1 + c]))
        load_enc[-1].start()
    load_mask = pltpu.make_async_copy(mask_hbm, mask, load_sems.at[3])
    load_mask.start()
    load_enc_bias = pltpu.make_async_copy(enc_bias_hbm, enc_bias.at[0], load_sems.at[4])
    load_enc_bias.start()
    load_dec = pltpu.make_async_copy(dec_hbm, dec, load_sems.at[5])
    load_dec.start()
    load_dec_bias = pltpu.make_async_copy(dec_bias_hbm, dec_bias.at[0], load_sems.at[6])
    load_dec_bias.start()

    @pl.when(odd)
    def _():
        for r in range(HALF):
            suffix[r, 0] = jnp.zeros((SUB, width), jnp.bfloat16)

    load_act.wait()
    swaps = []
    for c in range(2):
        load_enc[c].wait()
        part[:, halves[c]] = jnp.dot(act[...], enc[:, halves[c]], preferred_element_type=jnp.float32)
        if c == 0:
            pl.semaphore_wait(barrier, HALF + 1)
        here, there = part.at[:, sides[c]], part_in.at[:, sides[c]]
        swaps.append(remote(here, there, wid_sems.at[2 * c], wid_sems.at[2 * c + 1], other_core))
        swaps[-1].start()

    first = lat * block
    cut = jnp.int32(0)
    for k in range(GROUPS - 1):
        bound = bounds[k]
        cut = cut + jnp.where((bound > first) & (bound <= first + block), bound, 0)
    tokens = act.shape[0]
    below = (lax.broadcasted_iota(jnp.int32, (tokens, block), 1) + first) < cut
    load_mask.wait()
    load_enc_bias.wait()
    load_dec_bias.wait()
    kept = mask[...].astype(jnp.float32)
    load_dec.wait()
    for swap in swaps:
        swap.wait()
    full = kept * ((part[...] + part_in[...]) + enc_bias[...])
    low = jnp.where(below, full, 0.0).astype(jnp.bfloat16)
    high = jnp.where(below, 0.0, full).astype(jnp.bfloat16)
    for r in range(HALF):
        codes[2 * SUB * r : 2 * SUB * r + SUB, :] = low[SUB * r : SUB * (r + 1), :]
        codes[2 * SUB * r + SUB : 2 * SUB * (r + 1), :] = high[SUB * r : SUB * (r + 1), :]

    def send_pieces(c, step, both):
        target = peer(step)
        if both:
            src, dst = pieces_out.at[target, :, :, views[c]], pieces.at[place, :, :, views[c]]
        else:
            src, dst = pieces_out.at[target, 1, :, views[c]], pieces.at[place, 1, :, views[c]]
        return remote(src, dst, a_send.at[c, step], a_recv.at[c, place], device(target))

    def wait_pieces(c, step):
        origin = source(step)

        @pl.when(origin % 2 == 0)
        def _():
            ref = pieces.at[origin, :, :, views[c]]
            remote(ref, ref, a_send.at[c, step], a_recv.at[c, origin], device(origin)).wait_recv()

        @pl.when(origin % 2 == 1)
        def _():
            ref = pieces.at[origin, 1, :, views[c]]
            remote(ref, ref, a_send.at[c, step], a_recv.at[c, origin], device(origin)).wait_recv()

    def make(c):
        span = spans[c]
        made = jnp.dot(codes[...], dec[:, span], preferred_element_type=jnp.float32)
        pieces_out[:, :, :, span] = made.astype(jnp.bfloat16).reshape(HALF, 2, SUB, span.stop - span.start)

        @pl.when(even)
        def _():
            for step in range(1, HALF):
                send_pieces(c, step, True).start()

        @pl.when(odd)
        def _():
            for step in range(1, HALF):
                send_pieces(c, step, False).start()

        pieces[place, :, :, span] = pieces_out[place, :, :, span]

    crossing = []

    def cross(c):
        for step in range(1, HALF):
            wait_pieces(c, step)
        low0, seg = reduce_pieces(pieces, spans[c])
        plain = ((low0 + seg[0]) + seg[1]) + (seg[2] + seg[3])
        weighted = ((5.0 * low0 + 4.0 * seg[0]) + 3.0 * seg[1]) + (2.0 * seg[2] + seg[3])
        cross_out[:, spans[c]] = jnp.where(half == 0, plain, weighted).astype(jnp.bfloat16)
        crossing.append(
            remote(cross_out.at[:, views[c]], cross_in.at[:, views[c]], x_send.at[c], x_recv.at[c], other_half)
        )
        crossing[-1].start()

    def send_suffix(c, step, both):
        target = peer(step)
        if both:
            src, dst = tails.at[pl.ds(target // 2, 2), :, views[c]], suffix.at[place, :, :, views[c]]
        else:
            src, dst = tails.at[target // 2 + 1, :, views[c]], suffix.at[place, 1, :, views[c]]
        return remote(src, dst, b_send.at[c, step], b_recv.at[c, place], device(target))

    later = half.astype(jnp.float32)
    own_rows = pl.ds(pl.multiple_of(place * SUB, SUB), SUB)

    def finalize(c):
        span = spans[c]
        low0, seg = reduce_pieces(pieces, spans[c])
        crossing[c].wait_recv()
        got = cross_in[:, span].astype(jnp.float32)
        base = dec_bias[:, span] - act[own_rows, span].astype(jnp.float32)
        before = base + later * (got + low0)
        errors = []
        running = before
        for k in range(4):
            running = running + seg[k]
            errors.append(running)
        tail = jnp.where(half == 0, 5.0 * errors[3] + got, errors[3])
        scaled = [tail]
        for k in (2, 1, 0):
            tail = tail + errors[k]
            scaled.append(tail)
        scaled.append(tail + before)
        for k in range(5):
            tails[k, :, span] = (scaled[4 - k] / GROUPS).astype(jnp.bfloat16)
        row_out[:, span] = jnp.sum(scaled[3] / GROUPS, axis=0, keepdims=True)
        for step in range(1, HALF):

            @pl.when(peer(step) % 2 == 0)
            def _():
                send_suffix(c, step, True).start()

            @pl.when(peer(step) % 2 == 1)
            def _():
                send_suffix(c, step, False).start()

        suffix[place, :, :, span] = tails[pl.ds(place // 2, 2), :, span]

    for c in range(chunks):
        make(c)
    act_turned[...] = act[...].T
    stores = [pltpu.make_async_copy(act_turned, act_out, store_sems.at[1])]
    stores[0].start()
    codes_turned[...] = codes[...].T
    for c in range(chunks + 1):
        if c < chunks:
            cross(c)
        if c > 0:
            finalize(c - 1)

    def row_copy(step):
        return remote(row_out, rows.at[place], r_send.at[step], r_recv.at[place], device(peer(step)))

    for step in range(1, HALF):
        row_copy(step).start()
    rows[place] = row_out[...]

    below_parts = below.astype(jnp.float32).reshape(HALF, SUB, block) > 0.5
    back = [None, None]
    swaps_back = []

    def grad_columns(c):
        span = spans[c]
        both = suffix[:, :, :, span].reshape(2 * tokens, span.stop - span.start)
        dec_grad[:, span] = jnp.dot(codes_turned[...], both, preferred_element_type=jnp.float32).astype(jnp.bfloat16)
        stores.append(pltpu.make_async_copy(dec_grad.at[:, views[c]], dec_grad_out.at[:, views[c]], store_sems.at[5 + c]))
        stores[-1].start()

    for c in range(chunks):

        @pl.when(even)
        def _():
            for step in range(1, HALF):
                origin = source(step)
                ref = suffix.at[origin, :, :, views[c]]
                remote(ref, ref, b_send.at[c, step], b_recv.at[c, origin], device(origin)).wait_recv()

        @pl.when(odd)
        def _():
            for step in range(1, HALF):
                origin = source(step)
                ref = suffix.at[origin, 1, :, views[c]]
                remote(ref, ref, b_send.at[c, step], b_recv.at[c, origin], device(origin)).wait_recv()

        span = spans[c]
        both = suffix[:, :, :, span].reshape(2 * tokens, span.stop - span.start)
        for side in range(2):
            term = lax.dot_general(
                both, dec[halves[side], span], (((1,), (1,)), ((), ())), preferred_element_type=jnp.float32
            )
            back[side] = term if back[side] is None else back[side] + term
            if c == chunks - 1:
                pair = back[side].reshape(HALF, 2, SUB, block // 2)
                chosen = jnp.where(below_parts[:, :, halves[side]], pair[:, 0], pair[:, 1])
                grad[:, halves[side]] = chosen.reshape(tokens, block // 2)
                here, there = grad.at[:, sides[side]], grad_in.at[:, sides[side]]
                swaps_back.append(
                    remote(here, there, wid_sems.at[4 + 2 * side], wid_sems.at[5 + 2 * side], other_core)
                )
                swaps_back[-1].start()
        if c < chunks - 2:
            grad_columns(c)

    for c in range(chunks - 2, chunks):
        grad_columns(c)

    for step in range(1, HALF):
        origin = source(step)
        remote(row_out, rows.at[origin], r_send.at[step], r_recv.at[origin], device(origin)).wait_recv()
    summed = rows[0]
    for r in range(1, HALF):
        summed = summed + rows[r]
    final_out[...] = summed
    finish = remote(final_out, final_in, x_send.at[chunks], x_recv.at[chunks], other_half)
    finish.start()

    for swap in swaps_back:
        swap.wait()
    pre = kept * (grad[...] + grad_in[...])
    pre_low[...] = pre.astype(jnp.bfloat16)
    stores.append(pltpu.make_async_copy(pre_low, pre_out, store_sems.at[2]))
    stores[-1].start()
    enc_bias_row[...] = jnp.sum(pre, axis=0, keepdims=True)
    stores.append(pltpu.make_async_copy(enc_bias_row, enc_bias_out, store_sems.at[3]))
    stores[-1].start()

    for c in range(chunks):
        crossing[c].wait_send()

        @pl.when(even)
        def _():
            for step in range(1, HALF):
                send_pieces(c, step, True).wait_send()

        @pl.when(odd)
        def _():
            for step in range(1, HALF):
                send_pieces(c, step, False).wait_send()

        for step in range(1, HALF):

            @pl.when(peer(step) % 2 == 0)
            def _():
                send_suffix(c, step, True).wait_send()

            @pl.when(peer(step) % 2 == 1)
            def _():
                send_suffix(c, step, False).wait_send()

    for step in range(1, HALF):
        row_copy(step).wait_send()
    finish.wait()
    dec_bias_row[...] = jnp.where(half == 0, final_out[...], final_in[...])
    stores.append(pltpu.make_async_copy(dec_bias_row, dec_bias_out, store_sems.at[4]))
    stores[-1].start()
    for store in stores:
        store.wait()


def grads_kernel(
    act_hbm, pre_hbm, dec_grad_in, enc_bias_in, dec_bias_in,
    enc_out, dec_out, enc_bias_out, dec_bias_out,
    act, pre, enc_grad, dec_grad, load_sems, store_sems,
):
    part = act.shape[0] // PARTS
    rows_each = dec_grad.shape[0] // PARTS
    bands = [pl.ds(k * rows_each, rows_each) for k in range(PARTS)]
    moves = [
        pltpu.make_async_copy(dec_grad_in.at[band], dec_grad.at[band], load_sems.at[2 + k])
        for k, band in enumerate(bands)
    ]
    loads = [
        pltpu.make_async_copy(pre_hbm, pre, load_sems.at[0]),
        pltpu.make_async_copy(act_hbm, act, load_sems.at[1]),
    ]
    stores = [
        pltpu.make_async_copy(enc_bias_in.at[0], enc_bias_out, store_sems.at[0]),
        pltpu.make_async_copy(dec_bias_in.at[0], dec_bias_out, store_sems.at[1]),
    ]
    for copy in loads + moves + stores:
        copy.start()
    for load in loads:
        load.wait()
    for k in range(PARTS):
        span, view = slice(k * part, (k + 1) * part), pl.ds(k * part, part)
        enc_grad[span, :] = jnp.dot(act[span, :], pre[...], preferred_element_type=jnp.float32).astype(jnp.bfloat16)
        stores.append(pltpu.make_async_copy(enc_grad.at[view, :], enc_out.at[view, :], store_sems.at[2 + k]))
        stores[-1].start()
        moves[k].wait()
        stores.append(pltpu.make_async_copy(dec_grad.at[bands[k]], dec_out.at[bands[k]], store_sems.at[2 + PARTS + k]))
        stores[-1].start()
    for store in stores:
        store.wait()


def kernel_body(activations, encoder, encoder_bias, decoder, decoder_bias, kept_mask, boundaries):
    tokens, width = activations.shape
    block = encoder.shape[1]
    chunks = len(column_chunks(width))
    low, full = jnp.bfloat16, jnp.float32
    hbm = pl.BlockSpec(memory_space=pltpu.HBM)
    smem = pl.BlockSpec(memory_space=pltpu.SMEM)
    dma = pltpu.SemaphoreType.DMA
    act_turned, dec_grad, pre, enc_bias_grad, dec_bias_grad = pl.pallas_call(
        exchange_kernel,
        out_shape=[
            jax.ShapeDtypeStruct((width, tokens), low),
            jax.ShapeDtypeStruct((block, width), low),
            jax.ShapeDtypeStruct((tokens, block), low),
            jax.ShapeDtypeStruct((1, block), full),
            jax.ShapeDtypeStruct((1, width), full),
        ],
        in_specs=[hbm, hbm, hbm, hbm, hbm, hbm, smem],
        out_specs=[hbm, hbm, hbm, hbm, hbm],
        scratch_shapes=[
            pltpu.VMEM((tokens, width), low),
            pltpu.VMEM((width, block), low),
            pltpu.VMEM((1, block), full),
            pltpu.VMEM((block, width), low),
            pltpu.VMEM((1, width), full),
            pltpu.VMEM((tokens, block), jnp.int32),
            pltpu.VMEM((tokens, block), full),
            pltpu.VMEM((tokens, block), full),
            pltpu.VMEM((tokens, block), full),
            pltpu.VMEM((tokens, block), full),
            pltpu.VMEM((2 * tokens, block), low),
            pltpu.VMEM((HALF, 2, SUB, width), low),
            pltpu.VMEM((HALF, 2, SUB, width), low),
            pltpu.VMEM((SUB, width), low),
            pltpu.VMEM((SUB, width), low),
            pltpu.VMEM((5, SUB, width), low),
            pltpu.VMEM((HALF, 2, SUB, width), low),
            pltpu.VMEM((1, width), full),
            pltpu.VMEM((HALF, 1, width), full),
            pltpu.VMEM((1, width), full),
            pltpu.VMEM((1, width), full),
            pltpu.VMEM((tokens, block), low),
            pltpu.VMEM((1, block), full),
            pltpu.VMEM((1, width), full),
            pltpu.VMEM((width, tokens), low),
            pltpu.VMEM((block, 2 * tokens), low),
            pltpu.VMEM((block, width), low),
            dma((7,)),
            dma((8,)),
            dma((chunks, HALF)),
            dma((chunks, HALF)),
            dma((chunks + 1,)),
            dma((chunks + 1,)),
            dma((chunks, HALF)),
            dma((chunks, HALF)),
            dma((HALF,)),
            dma((HALF,)),
            dma((5 + chunks,)),
        ],
        compiler_params=pltpu.CompilerParams(
            collective_id=0, has_side_effects=True, vmem_limit_bytes=60 * 1024 * 1024
        ),
        name="exchange",
    )(
        activations, encoder, encoder_bias, decoder, decoder_bias, kept_mask, boundaries,
    )
    enc_grad, dec_grad, enc_bias_grad, dec_bias_grad = pl.pallas_call(
        grads_kernel,
        out_shape=[
            jax.ShapeDtypeStruct((width, block), low),
            jax.ShapeDtypeStruct((block, width), low),
            jax.ShapeDtypeStruct((block,), full),
            jax.ShapeDtypeStruct((width,), full),
        ],
        in_specs=[hbm] * 5,
        out_specs=[hbm] * 4,
        scratch_shapes=[
            pltpu.VMEM((width, tokens), low),
            pltpu.VMEM((tokens, block), low),
            pltpu.VMEM((width, block), low),
            pltpu.VMEM((block, width), low),
            dma((2 + PARTS,)),
            dma((2 + 2 * PARTS,)),
        ],
        compiler_params=pltpu.CompilerParams(vmem_limit_bytes=60 * 1024 * 1024),
        name="grads",
    )(act_turned, pre, dec_grad, enc_bias_grad, dec_bias_grad)
    return enc_grad, enc_bias_grad, dec_grad, dec_bias_grad


def fits(mesh):
    return mesh.shape["lat"] == 2 * HALF and mesh.shape["wid"] == 2


def solution(mesh):
    placed = (
        P(None, "wid"),
        P("wid", "lat"),
        P("lat"),
        P("lat", "wid"),
        P("wid"),
        P(None, "lat"),
        P(),
    )
    return jax.shard_map(
        kernel_body if fits(mesh) else general_body,
        mesh=mesh,
        in_specs=placed,
        out_specs=(P("wid", "lat"), P("lat"), P("lat", "wid"), P("wid")),
        check_vma=False,
    )
```

```python
import functools

import jax
import jax.numpy as jnp
from jax import lax
from jax.experimental import pallas as pl
from jax.experimental.pallas import tpu as pltpu
from jax.sharding import PartitionSpec as P

GROUPS = 8
HALF = 8
SUB = 16
LANES = 128
PARTS = 2
MESH = pl.DeviceIdType.MESH


def prefix(part, axis, combine, identity, reverse):
    count = lax.axis_size(axis)
    place = lax.axis_index(axis)
    ahead = count - 1 - place if reverse else place
    gathered = lax.all_gather(part, axis)
    state = jnp.zeros_like(part) + jnp.asarray(identity, part.dtype)

    def one(step, state):
        source = count - 1 - step if reverse else step
        return combine(state, lax.dynamic_index_in_dim(gathered, source, 0, False))

    return lax.fori_loop(0, ahead, one, state)


def add_terms(earlier, later):
    return earlier + later


def general_body(activations, encoder, encoder_bias, decoder, decoder_bias, kept_mask, boundaries):
    latent_width = encoder.shape[1]
    first_latent = lax.axis_index("lat") * latent_width
    latent_ids = first_latent + jnp.arange(latent_width, dtype=jnp.int32)
    kept_float = kept_mask.astype(jnp.float32)
    encoder_part = jnp.dot(activations, encoder, preferred_element_type=jnp.float32)
    preacts = lax.psum(encoder_part, "wid") + encoder_bias
    codes = (kept_float * preacts).astype(jnp.bfloat16)
    inside_rows = (boundaries > first_latent) & (boundaries <= first_latent + latent_width)
    holds_cut = jnp.any(inside_rows)
    cut_point = jnp.sum(jnp.where(inside_rows, boundaries, 0))
    below_cut = latent_ids < cut_point
    zero_code = jnp.zeros((), jnp.bfloat16)
    masked_codes = jnp.stack(
        [
            jnp.where(below_cut[None, :], codes, zero_code),
            jnp.where(below_cut[None, :], zero_code, codes),
        ]
    )
    decoded_pieces = jnp.einsum(
        "sbj,jd->sbd", masked_codes, decoder, preferred_element_type=jnp.float32
    )
    local_total = decoded_pieces[0] + decoded_pieces[1]
    zero_rows = jnp.zeros_like(local_total)
    prefix_sum = prefix(local_total, "lat", add_terms, zero_rows, False)
    target_rows = activations.astype(jnp.float32)
    scaled_error = jnp.where(
        holds_cut, (decoder_bias + prefix_sum + decoded_pieces[0] - target_rows) / GROUPS, 0.0
    )
    suffix_sum = prefix(scaled_error, "lat", add_terms, zero_rows, True)
    below_suffix = suffix_sum + scaled_error
    suffix_pair = jnp.stack([below_suffix, suffix_sum]).astype(jnp.bfloat16)
    back_grads = jnp.einsum("sbd,jd->sbj", suffix_pair, decoder, preferred_element_type=jnp.float32)
    partial_grads = jnp.where(below_cut[None, :], back_grads[0], back_grads[1])
    coded_grads = lax.psum(partial_grads, "wid")
    pre_grads = kept_float * coded_grads
    encoder_bias_grad = jnp.sum(pre_grads, axis=0)
    pre_low = pre_grads.astype(jnp.bfloat16)
    encoder_grad = lax.dot_general(
        activations, pre_low, (((0,), (0,)), ((), ())), preferred_element_type=jnp.float32
    ).astype(jnp.bfloat16)
    decoder_grad = jnp.einsum(
        "sbj,sbd->jd", masked_codes, suffix_pair, preferred_element_type=jnp.float32
    ).astype(jnp.bfloat16)
    decoder_bias_grad = lax.psum(jnp.sum(scaled_error, axis=0), "lat")
    return (encoder_grad, encoder_bias_grad, decoder_grad, decoder_bias_grad)


def column_chunks(width):
    tiles = width // LANES
    widths = []
    while tiles > 0:
        widths.append(min(4 if len(widths) in (1, 2) else 2, tiles))
        tiles -= widths[-1]
    ends = [LANES * sum(widths[: k + 1]) for k in range(len(widths))]
    return [slice(end - LANES * count, end) for end, count in zip(ends, widths)]


def reduce_pieces(pieces, span):
    def piece(source, which):
        return pieces[source, which, :, span].astype(jnp.float32)

    upper = [piece(2 * k, 1) + piece(2 * k + 1, 1) for k in range(4)]
    lower = [piece(2 * k, 0) for k in range(4)]
    segments = [upper[k] + lower[k + 1] for k in range(3)] + [upper[3]]
    return lower[0], segments


def exchange_kernel(
    act_hbm, enc_hbm, enc_bias_hbm, dec_hbm, dec_bias_hbm, mask_hbm, bounds,
    act_out, dec_grad_out, pre_out, enc_bias_out, dec_bias_out,
    act, enc, enc_bias, dec, dec_bias, mask, part, part_in, grad, grad_in, codes,
    pieces_out, pieces, cross_out, cross_in, tails, suffix,
    row_out, rows, final_out, final_in, pre_low, enc_bias_row, dec_bias_row,
    act_turned, codes_turned, dec_grad,
    load_sems, wid_sems, a_send, a_recv, x_send, x_recv, b_send, b_recv, r_send, r_recv, store_sems,
):
    lat = lax.axis_index("lat")
    wid = lax.axis_index("wid")
    half = lat // HALF
    place = lat % HALF
    even = place % 2 == 0
    odd = place % 2 == 1
    width = act.shape[1]
    spans = column_chunks(width)
    chunks = len(spans)
    views = [pl.ds(span.start, span.stop - span.start) for span in spans]
    block = dec.shape[0]
    halves = [slice(0, block // 2), slice(block // 2, block)]
    sides = [pl.ds(0, block // 2), pl.ds(block // 2, block // 2)]
    other_core = {"lat": lat, "wid": 1 - wid}
    other_half = {"lat": (lat + HALF) % (2 * HALF), "wid": wid}

    def peer(step):
        return (place + step) % HALF

    def source(step):
        return (place + HALF - step) % HALF

    def device(position):
        return {"lat": half * HALF + position, "wid": wid}

    def remote(src, dst, send, recv, target):
        return pltpu.make_async_remote_copy(
            src_ref=src, dst_ref=dst, send_sem=send, recv_sem=recv, device_id=target, device_id_type=MESH
        )

    barrier = pltpu.get_barrier_semaphore()
    for step in range(1, HALF):
        pl.semaphore_signal(barrier, inc=1, device_id=device(peer(step)), device_id_type=MESH)
    pl.semaphore_signal(barrier, inc=1, device_id=other_core, device_id_type=MESH)
    pl.semaphore_signal(barrier, inc=1, device_id=other_half, device_id_type=MESH)

    load_act = pltpu.make_async_copy(act_hbm, act, load_sems.at[0])
    load_act.start()
    load_enc = []
    for c in range(2):
        load_enc.append(pltpu.make_async_copy(enc_hbm.at[:, sides[c]], enc.at[:, sides[c]], load_sems.at[1 + c]))
        load_enc[-1].start()
    load_mask = pltpu.make_async_copy(mask_hbm, mask, load_sems.at[3])
    load_mask.start()
    load_enc_bias = pltpu.make_async_copy(enc_bias_hbm, enc_bias.at[0], load_sems.at[4])
    load_enc_bias.start()
    load_dec = pltpu.make_async_copy(dec_hbm, dec, load_sems.at[5])
    load_dec.start()
    load_dec_bias = pltpu.make_async_copy(dec_bias_hbm, dec_bias.at[0], load_sems.at[6])
    load_dec_bias.start()

    @pl.when(odd)
    def _():
        for r in range(HALF):
            suffix[r, 0] = jnp.zeros((SUB, width), jnp.bfloat16)

    load_act.wait()
    swaps = []
    for c in range(2):
        load_enc[c].wait()
        part[:, halves[c]] = jnp.dot(act[...], enc[:, halves[c]], preferred_element_type=jnp.float32)
        if c == 0:
            pl.semaphore_wait(barrier, HALF + 1)
        here, there = part.at[:, sides[c]], part_in.at[:, sides[c]]
        swaps.append(remote(here, there, wid_sems.at[2 * c], wid_sems.at[2 * c + 1], other_core))
        swaps[-1].start()

    first = lat * block
    cut = jnp.int32(0)
    for k in range(GROUPS - 1):
        bound = bounds[k]
        cut = cut + jnp.where((bound > first) & (bound <= first + block), bound, 0)
    tokens = act.shape[0]
    below = (lax.broadcasted_iota(jnp.int32, (tokens, block), 1) + first) < cut
    load_mask.wait()
    load_enc_bias.wait()
    load_dec_bias.wait()
    kept = mask[...].astype(jnp.float32)
    load_dec.wait()
    for swap in swaps:
        swap.wait()
    full = kept * ((part[...] + part_in[...]) + enc_bias[...])
    low = jnp.where(below, full, 0.0).astype(jnp.bfloat16)
    high = jnp.where(below, 0.0, full).astype(jnp.bfloat16)
    for r in range(HALF):
        codes[2 * SUB * r : 2 * SUB * r + SUB, :] = low[SUB * r : SUB * (r + 1), :]
        codes[2 * SUB * r + SUB : 2 * SUB * (r + 1), :] = high[SUB * r : SUB * (r + 1), :]

    def send_pieces(c, step, both):
        target = peer(step)
        if both:
            src, dst = pieces_out.at[target, :, :, views[c]], pieces.at[place, :, :, views[c]]
        else:
            src, dst = pieces_out.at[target, 1, :, views[c]], pieces.at[place, 1, :, views[c]]
        return remote(src, dst, a_send.at[c, step], a_recv.at[c, place], device(target))

    def wait_pieces(c, step):
        origin = source(step)

        @pl.when(origin % 2 == 0)
        def _():
            ref = pieces.at[origin, :, :, views[c]]
            remote(ref, ref, a_send.at[c, step], a_recv.at[c, origin], device(origin)).wait_recv()

        @pl.when(origin % 2 == 1)
        def _():
            ref = pieces.at[origin, 1, :, views[c]]
            remote(ref, ref, a_send.at[c, step], a_recv.at[c, origin], device(origin)).wait_recv()

    def make(c):
        span = spans[c]
        made = jnp.dot(codes[...], dec[:, span], preferred_element_type=jnp.float32)
        pieces_out[:, :, :, span] = made.astype(jnp.bfloat16).reshape(HALF, 2, SUB, span.stop - span.start)

        @pl.when(even)
        def _():
            for step in range(1, HALF):
                send_pieces(c, step, True).start()

        @pl.when(odd)
        def _():
            for step in range(1, HALF):
                send_pieces(c, step, False).start()

        pieces[place, :, :, span] = pieces_out[place, :, :, span]

    crossing = []

    def cross(c):
        for step in range(1, HALF):
            wait_pieces(c, step)
        low0, seg = reduce_pieces(pieces, spans[c])
        plain = ((low0 + seg[0]) + seg[1]) + (seg[2] + seg[3])
        weighted = ((5.0 * low0 + 4.0 * seg[0]) + 3.0 * seg[1]) + (2.0 * seg[2] + seg[3])
        cross_out[:, spans[c]] = jnp.where(half == 0, plain, weighted).astype(jnp.bfloat16)
        crossing.append(
            remote(cross_out.at[:, views[c]], cross_in.at[:, views[c]], x_send.at[c], x_recv.at[c], other_half)
        )
        crossing[-1].start()

    def send_suffix(c, step, both):
        target = peer(step)
        if both:
            src, dst = tails.at[pl.ds(target // 2, 2), :, views[c]], suffix.at[place, :, :, views[c]]
        else:
            src, dst = tails.at[target // 2 + 1, :, views[c]], suffix.at[place, 1, :, views[c]]
        return remote(src, dst, b_send.at[c, step], b_recv.at[c, place], device(target))

    later = half.astype(jnp.float32)
    own_rows = pl.ds(pl.multiple_of(place * SUB, SUB), SUB)

    def finalize(c):
        span = spans[c]
        low0, seg = reduce_pieces(pieces, spans[c])
        crossing[c].wait_recv()
        got = cross_in[:, span].astype(jnp.float32)
        base = dec_bias[:, span] - act[own_rows, span].astype(jnp.float32)
        before = base + later * (got + low0)
        errors = []
        running = before
        for k in range(4):
            running = running + seg[k]
            errors.append(running)
        tail = jnp.where(half == 0, 5.0 * errors[3] + got, errors[3])
        scaled = [tail]
        for k in (2, 1, 0):
            tail = tail + errors[k]
            scaled.append(tail)
        scaled.append(tail + before)
        for k in range(5):
            tails[k, :, span] = (scaled[4 - k] / GROUPS).astype(jnp.bfloat16)
        row_out[:, span] = jnp.sum(scaled[3] / GROUPS, axis=0, keepdims=True)
        for step in range(1, HALF):

            @pl.when(peer(step) % 2 == 0)
            def _():
                send_suffix(c, step, True).start()

            @pl.when(peer(step) % 2 == 1)
            def _():
                send_suffix(c, step, False).start()

        suffix[place, :, :, span] = tails[pl.ds(place // 2, 2), :, span]

    for c in range(chunks):
        make(c)
    act_turned[...] = act[...].T
    stores = [pltpu.make_async_copy(act_turned, act_out, store_sems.at[1])]
    stores[0].start()
    codes_turned[...] = codes[...].T
    for c in range(chunks + 1):
        if c < chunks:
            cross(c)
        if c > 0:
            finalize(c - 1)

    def row_copy(step):
        return remote(row_out, rows.at[place], r_send.at[step], r_recv.at[place], device(peer(step)))

    for step in range(1, HALF):
        row_copy(step).start()
    rows[place] = row_out[...]

    below_parts = below.astype(jnp.float32).reshape(HALF, SUB, block) > 0.5
    back = [None, None]
    swaps_back = []

    def grad_columns(c):
        span = spans[c]
        both = suffix[:, :, :, span].reshape(2 * tokens, span.stop - span.start)
        dec_grad[:, span] = jnp.dot(codes_turned[...], both, preferred_element_type=jnp.float32).astype(jnp.bfloat16)
        stores.append(pltpu.make_async_copy(dec_grad.at[:, views[c]], dec_grad_out.at[:, views[c]], store_sems.at[5 + c]))
        stores[-1].start()

    for c in range(chunks):

        @pl.when(even)
        def _():
            for step in range(1, HALF):
                origin = source(step)
                ref = suffix.at[origin, :, :, views[c]]
                remote(ref, ref, b_send.at[c, step], b_recv.at[c, origin], device(origin)).wait_recv()

        @pl.when(odd)
        def _():
            for step in range(1, HALF):
                origin = source(step)
                ref = suffix.at[origin, 1, :, views[c]]
                remote(ref, ref, b_send.at[c, step], b_recv.at[c, origin], device(origin)).wait_recv()

        span = spans[c]
        both = suffix[:, :, :, span].reshape(2 * tokens, span.stop - span.start)
        for side in range(2):
            term = lax.dot_general(
                both, dec[halves[side], span], (((1,), (1,)), ((), ())), preferred_element_type=jnp.float32
            )
            back[side] = term if back[side] is None else back[side] + term
            if c == chunks - 1:
                pair = back[side].reshape(HALF, 2, SUB, block // 2)
                chosen = jnp.where(below_parts[:, :, halves[side]], pair[:, 0], pair[:, 1])
                grad[:, halves[side]] = chosen.reshape(tokens, block // 2)
                here, there = grad.at[:, sides[side]], grad_in.at[:, sides[side]]
                swaps_back.append(
                    remote(here, there, wid_sems.at[4 + 2 * side], wid_sems.at[5 + 2 * side], other_core)
                )
                swaps_back[-1].start()
        if c < chunks - 2:
            grad_columns(c)

    for c in range(chunks - 2, chunks):
        grad_columns(c)

    for step in range(1, HALF):
        origin = source(step)
        remote(row_out, rows.at[origin], r_send.at[step], r_recv.at[origin], device(origin)).wait_recv()
    summed = rows[0]
    for r in range(1, HALF):
        summed = summed + rows[r]
    final_out[...] = summed
    finish = remote(final_out, final_in, x_send.at[chunks], x_recv.at[chunks], other_half)
    finish.start()

    for swap in swaps_back:
        swap.wait()
    pre = kept * (grad[...] + grad_in[...])
    pre_low[...] = pre.astype(jnp.bfloat16)
    stores.append(pltpu.make_async_copy(pre_low, pre_out, store_sems.at[2]))
    stores[-1].start()
    enc_bias_row[...] = jnp.sum(pre, axis=0, keepdims=True)
    stores.append(pltpu.make_async_copy(enc_bias_row, enc_bias_out, store_sems.at[3]))
    stores[-1].start()

    for c in range(chunks):
        crossing[c].wait_send()

        @pl.when(even)
        def _():
            for step in range(1, HALF):
                send_pieces(c, step, True).wait_send()

        @pl.when(odd)
        def _():
            for step in range(1, HALF):
                send_pieces(c, step, False).wait_send()

        for step in range(1, HALF):

            @pl.when(peer(step) % 2 == 0)
            def _():
                send_suffix(c, step, True).wait_send()

            @pl.when(peer(step) % 2 == 1)
            def _():
                send_suffix(c, step, False).wait_send()

    for step in range(1, HALF):
        row_copy(step).wait_send()
    finish.wait()
    dec_bias_row[...] = jnp.where(half == 0, final_out[...], final_in[...])
    stores.append(pltpu.make_async_copy(dec_bias_row, dec_bias_out, store_sems.at[4]))
    stores[-1].start()
    for store in stores:
        store.wait()


def grads_kernel(
    act_hbm, pre_hbm, dec_grad_in, enc_bias_in, dec_bias_in,
    enc_out, dec_out, enc_bias_out, dec_bias_out,
    act, pre, enc_grad, dec_grad, enc_bias, dec_bias, load_sems, store_sems,
):
    part = act.shape[0] // PARTS
    rows_each = dec_grad.shape[0] // PARTS
    bands = [pl.ds(k * rows_each, rows_each) for k in range(PARTS)]
    moves = [
        pltpu.make_async_copy(dec_grad_in.at[band], dec_grad.at[band], load_sems.at[2 + k])
        for k, band in enumerate(bands)
    ]
    loads = [
        pltpu.make_async_copy(pre_hbm, pre, load_sems.at[0]),
        pltpu.make_async_copy(act_hbm, act, load_sems.at[1]),
    ]
    biases = [
        pltpu.make_async_copy(enc_bias_in, enc_bias, load_sems.at[2 + PARTS]),
        pltpu.make_async_copy(dec_bias_in, dec_bias, load_sems.at[3 + PARTS]),
    ]
    stores = [
        pltpu.make_async_copy(enc_bias.at[0], enc_bias_out, store_sems.at[0]),
        pltpu.make_async_copy(dec_bias.at[0], dec_bias_out, store_sems.at[1]),
    ]
    for copy in loads + biases + moves:
        copy.start()
    for load in loads + biases:
        load.wait()
    for store in stores:
        store.start()
    for k in range(PARTS):
        span, view = slice(k * part, (k + 1) * part), pl.ds(k * part, part)
        enc_grad[span, :] = jnp.dot(act[span, :], pre[...], preferred_element_type=jnp.float32).astype(jnp.bfloat16)
        stores.append(pltpu.make_async_copy(enc_grad.at[view, :], enc_out.at[view, :], store_sems.at[2 + k]))
        stores[-1].start()
        moves[k].wait()
        stores.append(pltpu.make_async_copy(dec_grad.at[bands[k]], dec_out.at[bands[k]], store_sems.at[2 + PARTS + k]))
        stores[-1].start()
    for store in stores:
        store.wait()


def kernel_body(activations, encoder, encoder_bias, decoder, decoder_bias, kept_mask, boundaries):
    tokens, width = activations.shape
    block = encoder.shape[1]
    chunks = len(column_chunks(width))
    low, full = jnp.bfloat16, jnp.float32
    hbm = pl.BlockSpec(memory_space=pltpu.HBM)
    smem = pl.BlockSpec(memory_space=pltpu.SMEM)
    dma = pltpu.SemaphoreType.DMA
    act_turned, dec_grad, pre, enc_bias_grad, dec_bias_grad = pl.pallas_call(
        exchange_kernel,
        out_shape=[
            jax.ShapeDtypeStruct((width, tokens), low),
            jax.ShapeDtypeStruct((block, width), low),
            jax.ShapeDtypeStruct((tokens, block), low),
            jax.ShapeDtypeStruct((1, block), full),
            jax.ShapeDtypeStruct((1, width), full),
        ],
        in_specs=[hbm, hbm, hbm, hbm, hbm, hbm, smem],
        out_specs=[hbm, hbm, hbm, hbm, hbm],
        scratch_shapes=[
            pltpu.VMEM((tokens, width), low),
            pltpu.VMEM((width, block), low),
            pltpu.VMEM((1, block), full),
            pltpu.VMEM((block, width), low),
            pltpu.VMEM((1, width), full),
            pltpu.VMEM((tokens, block), jnp.int32),
            pltpu.VMEM((tokens, block), full),
            pltpu.VMEM((tokens, block), full),
            pltpu.VMEM((tokens, block), full),
            pltpu.VMEM((tokens, block), full),
            pltpu.VMEM((2 * tokens, block), low),
            pltpu.VMEM((HALF, 2, SUB, width), low),
            pltpu.VMEM((HALF, 2, SUB, width), low),
            pltpu.VMEM((SUB, width), low),
            pltpu.VMEM((SUB, width), low),
            pltpu.VMEM((5, SUB, width), low),
            pltpu.VMEM((HALF, 2, SUB, width), low),
            pltpu.VMEM((1, width), full),
            pltpu.VMEM((HALF, 1, width), full),
            pltpu.VMEM((1, width), full),
            pltpu.VMEM((1, width), full),
            pltpu.VMEM((tokens, block), low),
            pltpu.VMEM((1, block), full),
            pltpu.VMEM((1, width), full),
            pltpu.VMEM((width, tokens), low),
            pltpu.VMEM((block, 2 * tokens), low),
            pltpu.VMEM((block, width), low),
            dma((7,)),
            dma((8,)),
            dma((chunks, HALF)),
            dma((chunks, HALF)),
            dma((chunks + 1,)),
            dma((chunks + 1,)),
            dma((chunks, HALF)),
            dma((chunks, HALF)),
            dma((HALF,)),
            dma((HALF,)),
            dma((5 + chunks,)),
        ],
        compiler_params=pltpu.CompilerParams(
            collective_id=0, has_side_effects=True, vmem_limit_bytes=60 * 1024 * 1024
        ),
        name="exchange",
    )(
        activations, encoder, encoder_bias, decoder, decoder_bias, kept_mask, boundaries,
    )
    enc_grad, dec_grad, enc_bias_grad, dec_bias_grad = pl.pallas_call(
        grads_kernel,
        out_shape=[
            jax.ShapeDtypeStruct((width, block), low),
            jax.ShapeDtypeStruct((block, width), low),
            jax.ShapeDtypeStruct((block,), full),
            jax.ShapeDtypeStruct((width,), full),
        ],
        in_specs=[hbm] * 5,
        out_specs=[hbm] * 4,
        scratch_shapes=[
            pltpu.VMEM((width, tokens), low),
            pltpu.VMEM((tokens, block), low),
            pltpu.VMEM((width, block), low),
            pltpu.VMEM((block, width), low),
            pltpu.VMEM((1, block), full),
            pltpu.VMEM((1, width), full),
            dma((4 + PARTS,)),
            dma((2 + 2 * PARTS,)),
        ],
        compiler_params=pltpu.CompilerParams(vmem_limit_bytes=60 * 1024 * 1024),
        name="grads",
    )(act_turned, pre, dec_grad, enc_bias_grad, dec_bias_grad)
    return enc_grad, enc_bias_grad, dec_grad, dec_bias_grad


def fits(mesh):
    return mesh.shape["lat"] == 2 * HALF and mesh.shape["wid"] == 2


def solution(mesh):
    placed = (
        P(None, "wid"),
        P("wid", "lat"),
        P("lat"),
        P("lat", "wid"),
        P("wid"),
        P(None, "lat"),
        P(),
    )
    return jax.shard_map(
        kernel_body if fits(mesh) else general_body,
        mesh=mesh,
        in_specs=placed,
        out_specs=(P("wid", "lat"), P("lat"), P("lat", "wid"), P("wid")),
        check_vma=False,
    )
```
